32 devices in a mesh: batch: 8 (over z, y), seq: 4 (over x, core).
Axes of the slice: x: 2, y: 2, z: 4, core: 2. Of those that a mesh axis runs over, the one named last changes fastest.
Arguments:
- tokens: bfloat16 [8192, 1024], P(('batch', 'seq')), may hold values from -6 to 6
- cotangent: bfloat16 [8192, 1024], P(('batch', 'seq')), may hold values from -6 to 6
- w_project: float32 [1024, 4120], P(('batch', 'seq')), may hold values from -0.1875 to 0.1875
- w_mixout: float32 [2048, 1024], P(('batch', 'seq')), may hold values from -0.125 to 0.125
- w_gateup: float32 [1024, 4096], P(('batch', 'seq')), may hold values from -0.1875 to 0.1875
- w_down: float32 [2048, 1024], P(('batch', 'seq')), may hold values from -0.125 to 0.125
- gains: float32 [3584], P(('batch', 'seq')), may hold values from 0.5 to 1.5
- conv_params: float32 [5, 1792], P(None, ('batch', 'seq')), may hold values from -3 to 3
- head_params: float32 [3, 24], replicated, may hold values from -8 to 1.5
- mom_project: float32 [1024, 4120], P(('batch', 'seq')), may hold values from -32 to 32
- sec_project: float32 [1024, 4120], P(('batch', 'seq')), may hold values from 106.496 to 434.176
- mom_mixout: float32 [2048, 1024], P(('batch', 'seq')), may hold values from -32 to 32
- sec_mixout: float32 [2048, 1024], P(('batch', 'seq')), may hold values from 106.496 to 434.176
- mom_gateup: float32 [1024, 4096], P(('batch', 'seq')), may hold values from -32 to 32
- sec_gateup: float32 [1024, 4096], P(('batch', 'seq')), may hold values from 106.496 to 434.176
- mom_down: float32 [2048, 1024], P(('batch', 'seq')), may hold values from -32 to 32
- sec_down: float32 [2048, 1024], P(('batch', 'seq')), may hold values from 106.496 to 434.176
- mom_gains: float32 [3584], P(('batch', 'seq')), may hold values from -64 to 64
- sec_gains: float32 [3584], P(('batch', 'seq')), may hold values from 434.176 to 1720.32
- mom_conv: float32 [5, 1792], P(None, ('batch', 'seq')), may hold values from -64 to 64
- sec_conv: float32 [5, 1792], P(None, ('batch', 'seq')), may hold values from 434.176 to 1720.32
- mom_head: float32 [3, 24], replicated, may hold values from -192 to 192
- sec_head: float32 [3, 24], replicated, may hold values from 4096 to 16384
Outputs:
- out_block: bfloat16 [8192, 1024], P(('batch', 'seq'))
- grad_tokens: float32 [8192, 1024], P(('batch', 'seq'))
- next_mom_project: float32 [1024, 4120], P(('batch', 'seq'))
- next_sec_project: float32 [1024, 4120], P(('batch', 'seq'))
- next_w_project: float32 [1024, 4120], P(('batch', 'seq'))
- next_mom_mixout: float32 [2048, 1024], P(('batch', 'seq'))
- next_sec_mixout: float32 [2048, 1024], P(('batch', 'seq'))
- next_w_mixout: float32 [2048, 1024], P(('batch', 'seq'))
- next_mom_gateup: float32 [1024, 4096], P(('batch', 'seq'))
- next_sec_gateup: float32 [1024, 4096], P(('batch', 'seq'))
- next_w_gateup: float32 [1024, 4096], P(('batch', 'seq'))
- next_mom_down: float32 [2048, 1024], P(('batch', 'seq'))
- next_sec_down: float32 [2048, 1024], P(('batch', 'seq'))
- next_w_down: float32 [2048, 1024], P(('batch', 'seq'))
- next_mom_gains: float32 [3584], P(('batch', 'seq'))
- next_sec_gains: float32 [3584], P(('batch', 'seq'))
- next_w_gains: float32 [3584], P(('batch', 'seq'))
- next_mom_conv: float32 [5, 1792], P(None, ('batch', 'seq'))
- next_sec_conv: float32 [5, 1792], P(None, ('batch', 'seq'))
- next_w_conv: float32 [5, 1792], P(None, ('batch', 'seq'))
- next_mom_head: float32 [3, 24], replicated
- next_sec_head: float32 [3, 24], replicated
- next_w_head: float32 [3, 24], replicated
The draws below stay inside these ranges and needn't reach their ends.
All inputs are finite; a program needn't handle non-finite values.
Results may differ from the reference program's by a relative error of at most 0.015.
The reference program's roundings to bfloat16 on the way count: a program that leaves them out, or rounds other values in their place, can miss the bound.
Values may be sent and summed in bfloat16 or wider, within the bound.
A program may use at most 192 MiB of HBM per device.

```python
import math
import jax
import jax.numpy as jnp
from jax import lax

D = 1024
FF = 2048
HEADS = 8
KV_HEADS = 2
HEAD_DIM = 64
M_HEADS = 24
M_DIM = 64
STATE = 128
CONV = 4
STEP = 10
LENGTH = 1024
SEQS = 8
TOKENS = 8192
QW = 512
KW = 128
M_INNER = 1536
CONV_CH = 1792
IN_COLS = 4120
MIX_ROWS = 2048
GAIN_LEN = 3584


def draw_head_params(key, part):
    key = jax.random.fold_in(key, 23)
    key_bias, key_slow, key_fast, key_pick, key_skip = jax.random.split(key, 5)
    step_bias = jax.random.uniform(key_bias, (M_HEADS,), jnp.float32, -4.0, -2.5)
    slow_rate = jnp.exp(jax.random.uniform(key_slow, (M_HEADS,), jnp.float32, math.log(3.0 / LENGTH), math.log(40.0 / LENGTH)))
    fast_rate = jnp.exp(jax.random.uniform(key_fast, (M_HEADS,), jnp.float32, math.log(0.5), math.log(1.5)))
    picked = jax.random.randint(key_pick, (M_HEADS,), 0, 2)
    decay_rate = jnp.where(picked == 1, fast_rate, slow_rate)
    skip_factor = jax.random.uniform(key_skip, (M_HEADS,), jnp.float32, 0.5, 1.5)
    return jnp.stack([step_bias, jnp.log(decay_rate), skip_factor])


def levels(stream_key, shape, cuts, smallest, high):
    gain, own = 1.0, jax.random.fold_in(stream_key, 6)
    for dim, parts in cuts:
        draws = jnp.exp(jax.random.uniform(jax.random.fold_in(own, dim), (parts,), jnp.float32, smallest / len(cuts), high / len(cuts)))
        gain = gain * jnp.repeat(draws, shape[dim] // parts).reshape([-1 if axis == dim else 1 for axis in range(len(shape))])
    return gain


def scatter_about(rng, shape, deviation, most, cuts=(), kind=jnp.bfloat16):
    result = deviation * jax.random.normal(rng, shape, jnp.float32)
    if cuts:
        result = result * levels(rng, shape, cuts, -0.22, 0.18)
    return jnp.clip(result, -most, most).astype(kind)


def setup_inputs(seed: int = 0) -> dict:
    key_list = jax.random.split(jax.random.key(seed), 24)
    tokens = scatter_about(key_list[0], (TOKENS, D), 1.0, 6.0, ((0, 32),))
    cotangent = scatter_about(key_list[1], (TOKENS, D), 1.0, 6.0, ((0, 32),))
    w_project = scatter_about(key_list[2], (D, IN_COLS), D ** -0.5, 0.1875, ((0, 32),), jnp.float32)
    w_mixout = scatter_about(key_list[3], (MIX_ROWS, D), MIX_ROWS ** -0.5, 0.125, ((0, 32),), jnp.float32)
    w_gateup = scatter_about(key_list[4], (D, 2 * FF), D ** -0.5, 0.1875, ((0, 32),), jnp.float32)
    w_down = scatter_about(key_list[5], (FF, D), FF ** -0.5, 0.125, ((0, 32),), jnp.float32)
    gains = jnp.clip(1.0 + 0.1 * jax.random.normal(key_list[6], (GAIN_LEN,), jnp.float32), 0.5, 1.5)
    conv_params = scatter_about(key_list[7], (CONV + 1, CONV_CH), 0.5, 3.0, ((1, 32),), jnp.float32)
    head_params = draw_head_params(jax.random.fold_in(key_list[23], 71), 0)
    mom_project = scatter_about(key_list[9], (D, IN_COLS), (0.055 * TOKENS ** 0.5), 32.0, ((0, 32),), jnp.float32)
    sec_project = jnp.clip(jnp.exp(math.log(434.176) - 1.40534252 * jax.random.uniform(key_list[10], (D, IN_COLS), jnp.float32) ** levels(key_list[10], (D, IN_COLS), ((0, 32),), -0.2, 0.2)), 106.496, 434.176)
    mom_mixout = scatter_about(key_list[11], (MIX_ROWS, D), (0.055 * TOKENS ** 0.5), 32.0, ((0, 32),), jnp.float32)
    sec_mixout = jnp.clip(jnp.exp(math.log(434.176) - 1.40534252 * jax.random.uniform(key_list[12], (MIX_ROWS, D), jnp.float32) ** levels(key_list[12], (MIX_ROWS, D), ((0, 32),), -0.2, 0.2)), 106.496, 434.176)
    mom_gateup = scatter_about(key_list[13], (D, 2 * FF), (0.055 * TOKENS ** 0.5), 32.0, ((0, 32),), jnp.float32)
    sec_gateup = jnp.clip(jnp.exp(math.log(434.176) - 1.40534252 * jax.random.uniform(key_list[14], (D, 2 * FF), jnp.float32) ** levels(key_list[14], (D, 2 * FF), ((0, 32),), -0.2, 0.2)), 106.496, 434.176)
    mom_down = scatter_about(key_list[15], (FF, D), (0.055 * TOKENS ** 0.5), 32.0, ((0, 32),), jnp.float32)
    sec_down = jnp.clip(jnp.exp(math.log(434.176) - 1.40534252 * jax.random.uniform(key_list[16], (FF, D), jnp.float32) ** levels(key_list[16], (FF, D), ((0, 32),), -0.2, 0.2)), 106.496, 434.176)
    mom_gains = scatter_about(key_list[17], (GAIN_LEN,), (0.11 * TOKENS ** 0.5), 64.0, ((0, 32),), jnp.float32)
    sec_gains = jnp.clip(jnp.exp(math.log(1720.32) - 1.3768156 * jax.random.uniform(key_list[18], (GAIN_LEN,), jnp.float32) ** levels(key_list[18], (GAIN_LEN,), ((0, 32),), -0.2, 0.2)), 434.176, 1720.32)
    mom_conv = scatter_about(key_list[19], (CONV + 1, CONV_CH), (0.11 * TOKENS ** 0.5), 64.0, ((1, 32),), jnp.float32)
    sec_conv = jnp.clip(jnp.exp(math.log(1720.32) - 1.3768156 * jax.random.uniform(key_list[20], (CONV + 1, CONV_CH), jnp.float32) ** levels(key_list[20], (CONV + 1, CONV_CH), ((1, 32),), -0.2, 0.2)), 434.176, 1720.32)
    mom_head = scatter_about(key_list[21], (3, M_HEADS), (0.33 * TOKENS ** 0.5), 192.0, (), jnp.float32)
    sec_head = jnp.clip(jnp.exp(jax.random.uniform(key_list[22], (3, M_HEADS), jnp.float32, math.log(4096.0), math.log(16384.0))), 4096.0, 16384.0)
    return dict(tokens=tokens, cotangent=cotangent, w_project=w_project, w_mixout=w_mixout, w_gateup=w_gateup, w_down=w_down, gains=gains, conv_params=conv_params, head_params=head_params, mom_project=mom_project, sec_project=sec_project, mom_mixout=mom_mixout, sec_mixout=sec_mixout, mom_gateup=mom_gateup, sec_gateup=sec_gateup, mom_down=mom_down, sec_down=sec_down, mom_gains=mom_gains, sec_gains=sec_gains, mom_conv=mom_conv, sec_conv=sec_conv, mom_head=mom_head, sec_head=sec_head)


epsilon = 1e-05
rope_base = 100000000000.0
beta_one = 0.9
beta_two = 0.95
adam_eps = 1e-08
weight_decay = 0.1
rate_matrix = 0.06
rate_vector = 1.0
highest = lax.Precision.HIGHEST

@jax.custom_vjp
def low(v):
    return lax.optimization_barrier(v.astype(jnp.bfloat16)).astype(jnp.float32)

@jax.custom_vjp
def low_back(v):
    return v

def low_keep(v):
    return (low(v), None)

def low_pass(kept, grad):
    return (grad,)

def back_keep(v):
    return (v, None)

def back_low(kept, grad):
    return (low(grad),)
low.defvjp(low_keep, low_pass)
low_back.defvjp(back_keep, back_low)

def matmul(left, right):
    return jnp.dot(left, right, precision=highest, preferred_element_type=jnp.float32)

def rms_scale(values, gain_vector):
    return values * lax.rsqrt(lax.optimization_barrier(jnp.mean(values * values, axis=-1, keepdims=True)) + epsilon) * gain_vector

def rope_tables(positions):
    half_dim = HEAD_DIM // 2
    frequency = jnp.power(rope_base, -2.0 * jnp.arange(half_dim, dtype=jnp.float32) / HEAD_DIM)
    angles = positions.astype(jnp.float32)[:, None] * frequency[None, :]
    return (jnp.cos(angles)[:, None, :], jnp.sin(angles)[:, None, :])

def rotate(heads, cosine, sine_table):
    half_dim = HEAD_DIM // 2
    first_half = heads[..., :half_dim]
    second_half = heads[..., half_dim:]
    return jnp.concatenate([first_half * cosine - second_half * sine_table, second_half * cosine + first_half * sine_table], axis=-1)

def prepare(padded, conv_taps, head_params, dt_raw):
    row_count = dt_raw.shape[0]
    summed = conv_taps[CONV]
    for tap_index in range(CONV):
        summed = summed + conv_taps[tap_index] * padded[tap_index:tap_index + row_count]
    activated = jax.nn.silu(summed)
    x_heads = activated[:, :M_INNER].reshape(row_count, M_HEADS, M_DIM)
    b_matrix = activated[:, M_INNER:M_INNER + STATE]
    c_matrix = activated[:, M_INNER + STATE:]
    step_size = jax.nn.softplus(dt_raw + head_params[0])
    log_decay = -step_size * jnp.exp(head_params[1])
    return (step_size[:, :, None] * x_heads, log_decay, b_matrix, c_matrix, x_heads)

def ssm_span(state_in, pieces):
    inputs, log_decay, b_matrix, c_matrix = pieces
    count_rows = log_decay.shape[0]
    cumulated = jnp.cumsum(log_decay, axis=0)
    lower_mask = (jnp.arange(count_rows)[:, None] >= jnp.arange(count_rows)[None, :])[:, :, None]
    log_gaps = jnp.where(lower_mask, cumulated[:, None, :] - cumulated[None, :, :], -1e+30)
    mixing = matmul(c_matrix, b_matrix.T)[:, :, None] * jnp.exp(log_gaps)
    within = jnp.einsum('tsh,shp->thp', mixing, inputs, precision=highest)
    carried = jnp.einsum('tn,hpn->thp', c_matrix, state_in, precision=highest) * jnp.exp(cumulated)[:, :, None]
    tail_decay = jnp.exp(cumulated[-1][None, :] - cumulated)
    state_out = state_in * jnp.exp(cumulated[-1])[:, None, None] + jnp.einsum('shp,sn->hpn', tail_decay[:, :, None] * inputs, b_matrix, precision=highest)
    return (state_out, within + carried)

def mamba_mixer(xbc_raw, dt_raw, gate_z, conv_taps, head_params, gain_vector):
    padded = jnp.concatenate([jnp.zeros((CONV - 1, CONV_CH), jnp.float32), xbc_raw], axis=0)
    inputs, log_decay, b_matrix, c_matrix, x_heads = prepare(padded, conv_taps, head_params, dt_raw)
    span_len = min(256, LENGTH)
    count_spans = LENGTH // span_len
    pieces = (inputs.reshape(count_spans, span_len, M_HEADS, M_DIM), log_decay.reshape(count_spans, span_len, M_HEADS), b_matrix.reshape(count_spans, span_len, STATE), c_matrix.reshape(count_spans, span_len, STATE))
    start_state = jnp.zeros((M_HEADS, M_DIM, STATE), jnp.float32)
    final_state, outputs = lax.scan(jax.checkpoint(ssm_span), start_state, pieces)
    output = outputs.reshape(LENGTH, M_HEADS, M_DIM) + head_params[2][None, :, None] * x_heads
    gated = output.reshape(LENGTH, M_INNER) * jax.nn.silu(gate_z)
    return rms_scale(gated, gain_vector)

def attention(queries, key_rows, value_rows):
    group_size = HEADS // KV_HEADS
    block_rows = min(512, LENGTH)
    keys_all = jnp.repeat(key_rows, group_size, axis=1)
    values_all = jnp.repeat(value_rows, group_size, axis=1)
    key_pos = jnp.arange(LENGTH, dtype=jnp.int32)

    def one_block(start_row):
        query_rows = lax.dynamic_slice_in_dim(queries, start_row, block_rows, 0)
        scores = jnp.einsum('qhd,khd->hqk', query_rows, keys_all, precision=highest)
        scores = low_back(scores * HEAD_DIM ** (-0.5))
        query_pos = start_row + jnp.arange(block_rows, dtype=jnp.int32)
        allowed = key_pos[None, :] <= query_pos[:, None]
        scores = jnp.where(allowed[None], scores, -1e+30)
        row_top = lax.optimization_barrier(jnp.max(scores, axis=-1, keepdims=True))
        weights = jnp.exp(scores - row_top)
        probability = weights / lax.optimization_barrier(jnp.sum(weights, axis=-1, keepdims=True))
        return jnp.einsum('hqk,khd->qhd', low(probability), values_all, precision=highest)
    starts = (jnp.arange(LENGTH // block_rows) * block_rows).astype(jnp.int32)
    outputs = lax.map(jax.checkpoint(one_block), starts)
    return outputs.reshape(LENGTH, QW)

def layer_forward(sequence, params):
    w_project, w_mixout, w_gateup, w_down, gains, conv_taps, head_params = params
    out_multiplier = (LENGTH / 6.0) ** 0.5
    normed = low(rms_scale(sequence, gains[:D]))
    projected = low_back(matmul(normed, w_project))
    cosine, sine_table = rope_tables(jnp.arange(LENGTH, dtype=jnp.int32))
    queries = low(rotate(projected[:, :QW].reshape(LENGTH, HEADS, HEAD_DIM), cosine, sine_table))
    key_rows = low(rotate(projected[:, QW:QW + KW].reshape(LENGTH, KV_HEADS, HEAD_DIM), cosine, sine_table))
    value_rows = low(projected[:, QW + KW:QW + 2 * KW].reshape(LENGTH, KV_HEADS, HEAD_DIM))
    attended = low_back(low(out_multiplier * attention(queries, key_rows, value_rows)))
    offset_cols = QW + 2 * KW
    mamba_out = mamba_mixer(projected[:, offset_cols + M_INNER:offset_cols + M_INNER + CONV_CH], projected[:, offset_cols + M_INNER + CONV_CH:], projected[:, offset_cols:offset_cols + M_INNER], conv_taps, head_params, gains[2 * D:])
    joined = jnp.concatenate([attended, low(mamba_out)], axis=1)
    hidden = sequence + low_back(matmul(joined, w_mixout))
    normed2 = low(rms_scale(hidden, gains[D:2 * D]))
    gate_up = low_back(matmul(normed2, w_gateup))
    activated = low(jax.nn.silu(gate_up[:, :FF]) * gate_up[:, FF:])
    return hidden + low_back(matmul(activated, w_down))

def adamw_update(weight, gradient, moment_one, moment_two, rate, decay):
    moment_one = beta_one * moment_one + (1.0 - beta_one) * gradient
    moment_two = beta_two * moment_two + (1.0 - beta_two) * gradient * gradient
    corrected_one = moment_one / (1.0 - beta_one ** STEP)
    corrected_two = moment_two / (1.0 - beta_two ** STEP)
    new_weight = weight - rate * (corrected_one / (jnp.sqrt(corrected_two) + adam_eps) + decay * weight)
    return (moment_one, moment_two, new_weight)

def reference(tokens, cotangent, w_project, w_mixout, w_gateup, w_down, gains, conv_params, head_params, mom_project, sec_project, mom_mixout, sec_mixout, mom_gateup, sec_gateup, mom_down, sec_down, mom_gains, sec_gains, mom_conv, sec_conv, mom_head, sec_head):

    def forward(tokens_f, wp_full, wm_full, wgu_full, wd_full, gain_full, conv_full, head_full):
        params = (low(wp_full), low(wm_full), low(wgu_full), low(wd_full), low(gain_full), low(conv_full), head_full)
        sequences = tokens_f.reshape(SEQS, LENGTH, D)
        layer_step = jax.checkpoint(layer_forward)
        outputs = lax.map(lambda sequence: layer_step(sequence, params), sequences)
        return outputs.reshape(TOKENS, D)
    block_f, pull_all = jax.vjp(forward, tokens.astype(jnp.float32), w_project, w_mixout, w_gateup, w_down, gains, conv_params, head_params)
    grads = pull_all(cotangent.astype(jnp.float32))
    g_tokens, g_project, g_mixout, g_gateup, g_down, g_gains, g_conv, g_head = grads
    r_project = adamw_update(w_project, g_project, mom_project, sec_project, rate_matrix, weight_decay)
    r_mixout = adamw_update(w_mixout, g_mixout, mom_mixout, sec_mixout, rate_matrix, weight_decay)
    r_gateup = adamw_update(w_gateup, g_gateup, mom_gateup, sec_gateup, rate_matrix, weight_decay)
    r_down = adamw_update(w_down, g_down, mom_down, sec_down, rate_matrix, weight_decay)
    r_gains = adamw_update(gains, g_gains, mom_gains, sec_gains, rate_vector, 0.0)
    r_conv = adamw_update(conv_params, g_conv, mom_conv, sec_conv, rate_vector, 0.0)
    r_head = adamw_update(head_params, g_head, mom_head, sec_head, rate_vector, 0.0)
    return (block_f.astype(jnp.bfloat16), g_tokens, r_project[0], r_project[1], r_project[2], r_mixout[0], r_mixout[1], r_mixout[2], r_gateup[0], r_gateup[1], r_gateup[2], r_down[0], r_down[1], r_down[2], r_gains[0], r_gains[1], r_gains[2], r_conv[0], r_conv[1], r_conv[2], r_head[0], r_head[1], r_head[2])
```

```python
import jax
import jax.numpy as jnp
from jax import lax
from jax.sharding import PartitionSpec as P

D = 1024
FF = 2048
HEADS = 8
KV_HEADS = 2
HEAD_DIM = 64
M_HEADS = 24
M_DIM = 64
STATE = 128
CONV = 4
STEP = 10


epsilon = 1e-05
rope_base = 100000000000.0
beta_one = 0.9
beta_two = 0.95
adam_eps = 1e-08
weight_decay = 0.1
rate_matrix = 0.06
rate_vector = 1.0
highest = lax.Precision.HIGHEST


def from_behind(value, axis, by):
    length = lax.axis_size(axis)
    pairs = [(i, i + by) for i in range(length) if 0 <= i + by < length]
    return lax.ppermute(value, axis, pairs)


def entering(value, axis, join, neutral):
    place = lax.axis_index(axis)
    gathered = jax.tree.map(
        lambda a, kind: lax.all_gather(a.astype(kind), axis), value, (jnp.bfloat16, jnp.bfloat16)
    )
    state = jax.tree.map(lambda a, e: jnp.zeros_like(a) + jnp.asarray(e, a.dtype), value, neutral)

    def one(turn, state):
        return join(
            state,
            jax.tree.map(
                lambda a, own: lax.dynamic_index_in_dim(a, turn, 0, False).astype(own.dtype),
                gathered,
                value,
            ),
        )

    return lax.fori_loop(0, place, one, state)


def entering_2(value, axis, combine, identity):
    length, index = (lax.axis_size(axis), lax.axis_index(axis))
    everything = jax.tree.map(
        lambda part, kind: lax.all_gather(part.astype(kind), axis),
        value,
        jax.tree.map(lambda a: jnp.bfloat16 if a.dtype == jnp.float32 else a.dtype, value),
    )
    start = jax.tree.map(
        lambda part, zero: jnp.broadcast_to(jnp.asarray(zero, part.dtype), part.shape),
        value,
        identity,
    )

    def turn(k, before):
        at = length - 1 - k
        reached = at > index
        new = combine(
            before, jax.tree.map(lambda part, own: part[at].astype(own.dtype), everything, value)
        )
        return jax.tree.map(lambda a, b: jnp.where(reached, a, b), new, before)

    return lax.fori_loop(0, length, turn, start)


def hp_matmul(left, right):
    return jnp.dot(left, right, precision=highest, preferred_element_type=jnp.float32)


def rms_scale(values, gain_vector):
    return (
        values
        * lax.rsqrt(jnp.mean(values * values, axis=-1, keepdims=True) + epsilon)
        * gain_vector
    )


def rope_tables(positions):
    half_dim = HEAD_DIM // 2
    frequency = jnp.power(rope_base, -2.0 * jnp.arange(half_dim, dtype=jnp.float32) / HEAD_DIM)
    angles = positions.astype(jnp.float32)[:, None] * frequency[None, :]
    return (jnp.cos(angles)[:, None, :], jnp.sin(angles)[:, None, :])


def rotate(heads, cosine, sine_table):
    half_dim = HEAD_DIM // 2
    first_half = heads[..., :half_dim]
    second_half = heads[..., half_dim:]
    return jnp.concatenate(
        [
            first_half * cosine - second_half * sine_table,
            second_half * cosine + first_half * sine_table,
        ],
        axis=-1,
    )


def prepare(padded, conv_taps, head_params, dt_raw):
    row_count = dt_raw.shape[0]
    inner_width = M_HEADS * M_DIM
    summed = conv_taps[CONV]
    for tap_index in range(CONV):
        summed = summed + conv_taps[tap_index] * padded[tap_index : tap_index + row_count]
    activated = jax.nn.silu(summed)
    x_heads = activated[:, :inner_width].reshape(row_count, M_HEADS, M_DIM)
    b_matrix = activated[:, inner_width : inner_width + STATE]
    c_matrix = activated[:, inner_width + STATE :]
    step_size = jax.nn.softplus(dt_raw + head_params[0])
    log_decay = -step_size * jnp.exp(head_params[1])
    return (step_size[:, :, None] * x_heads, log_decay, b_matrix, c_matrix, x_heads)


def local_state(inputs, log_decay, b_matrix):
    cumulated = jnp.cumsum(log_decay, axis=0)
    tail_decay = jnp.exp(cumulated[-1][None, :] - cumulated)
    end_state = jnp.einsum(
        "shp,sn->hpn", tail_decay[:, :, None] * inputs, b_matrix, precision=highest
    )
    return (jnp.exp(cumulated[-1]), end_state)


def mamba_output(
    inputs, log_decay, b_matrix, c_matrix, x_heads, gate_z, head_params, gain_vector, start_state
):
    row_count = log_decay.shape[0]
    cumulated = jnp.cumsum(log_decay, axis=0)
    lower_mask = (jnp.arange(row_count)[:, None] >= jnp.arange(row_count)[None, :])[:, :, None]
    log_gaps = jnp.where(lower_mask, cumulated[:, None, :] - cumulated[None, :, :], -1e30)
    mixing = hp_matmul(c_matrix, b_matrix.T)[:, :, None] * jnp.exp(log_gaps)
    within = jnp.einsum("tsh,shp->thp", mixing, inputs, precision=highest)
    carried = (
        jnp.einsum("tn,hpn->thp", c_matrix, start_state, precision=highest)
        * jnp.exp(cumulated)[:, :, None]
    )
    output = within + carried + head_params[2][None, :, None] * x_heads
    gated = output.reshape(row_count, M_HEADS * M_DIM) * jax.nn.silu(gate_z)
    return rms_scale(gated, gain_vector)


def chain_step(earlier, later):
    return (earlier[0] * later[0], later[0][:, None, None] * earlier[1] + later[1])


def swiglu(gate_up):
    return jax.nn.silu(gate_up[:, :FF]) * gate_up[:, FF:]


def adamw_update(weight, gradient, moment_one, moment_two, rate, decay):
    moment_one = beta_one * moment_one + (1.0 - beta_one) * gradient
    moment_two = beta_two * moment_two + (1.0 - beta_two) * gradient * gradient
    corrected_one = moment_one / (1.0 - beta_one**STEP)
    corrected_two = moment_two / (1.0 - beta_two**STEP)
    new_weight = weight - rate * (
        corrected_one / (jnp.sqrt(corrected_two) + adam_eps) + decay * weight
    )
    return (moment_one, moment_two, new_weight)


def pack_project(weights, gains, taps):
    rows = weights.shape[0]
    vectors = jnp.concatenate([gains, taps.reshape(-1)])
    width = -(-vectors.shape[0] // rows)
    vectors = jnp.pad(vectors, (0, width * rows - vectors.shape[0])).reshape(rows, width)
    return jnp.concatenate([weights, vectors], axis=1).astype(jnp.bfloat16)


def pack_late(weights, gains, taps, devices):
    rows = weights.shape[0] // devices
    split_taps = jnp.transpose(taps.reshape(CONV + 1, devices, -1), (1, 0, 2))
    vectors = jnp.concatenate([gains.reshape(devices, -1), split_taps.reshape(devices, -1)], axis=1)
    width = -(-vectors.shape[1] // rows)
    vectors = jnp.pad(vectors, ((0, 0), (0, width * rows - vectors.shape[1])))
    return jnp.concatenate([weights, vectors.reshape(devices * rows, width)], axis=1).astype(
        jnp.bfloat16
    )


def unpack_vectors(packed, start, devices, gains, taps):
    vectors = packed[:, start:].reshape(devices, -1)
    count = gains.shape[0]
    own_gains = vectors[:, :count].reshape(-1)
    own_taps = vectors[:, count : count + taps.size].reshape(devices, CONV + 1, taps.shape[1])
    return own_gains, jnp.transpose(own_taps, (1, 0, 2)).reshape(CONV + 1, -1)


def local(
    tokens,
    cotangent,
    w_project,
    w_mixout,
    w_gateup,
    w_down,
    gains,
    conv_params,
    head_params,
    mom_project,
    sec_project,
    mom_mixout,
    sec_mixout,
    mom_gateup,
    sec_gateup,
    mom_down,
    sec_down,
    mom_gains,
    sec_gains,
    mom_conv,
    sec_conv,
    mom_head,
    sec_head,
):
    row_count = tokens.shape[0]
    group_size = HEADS // KV_HEADS
    scale_factor = HEAD_DIM ** (-0.5)
    q_width = HEADS * HEAD_DIM
    kv_width = KV_HEADS * HEAD_DIM
    inner_width = M_HEADS * M_DIM
    conv_width = inner_width + 2 * STATE
    offset_cols = q_width + 2 * kv_width
    out_multiplier = (row_count * lax.axis_size("seq") / 6.0) ** 0.5
    devices = lax.axis_size("batch") * lax.axis_size("seq")
    share = w_project.shape[0]
    full_packed = lax.all_gather(
        pack_project(w_project, gains, conv_params), ("batch", "seq"), axis=0, tiled=True
    )
    full_project = full_packed[:, : w_project.shape[1]]
    full_gains, full_conv = unpack_vectors(full_packed, w_project.shape[1], devices, gains, conv_params)
    full_mixout, full_gateup, full_down = (
        lax.all_gather(w_mixout.astype(jnp.bfloat16), ("batch", "seq"), axis=0, tiled=True),
        lax.all_gather(w_gateup.astype(jnp.bfloat16), ("batch", "seq"), axis=0, tiled=True),
        lax.all_gather(w_down.astype(jnp.bfloat16), ("batch", "seq"), axis=0, tiled=True),
    )
    gains_f = full_gains.astype(jnp.float32)
    gain_first = gains_f[:D]
    gain_second = gains_f[D : 2 * D]
    gain_mamba = gains_f[2 * D :]
    conv_taps = full_conv.astype(jnp.float32)
    tokens_f = tokens.astype(jnp.float32)
    normed_f, pull_first = jax.vjp(rms_scale, tokens_f, gain_first)
    normed = normed_f.astype(jnp.bfloat16)
    projected = jnp.dot(normed, full_project, preferred_element_type=jnp.float32)
    seq_index = lax.axis_index("seq")
    positions = seq_index * row_count + jnp.arange(row_count, dtype=jnp.int32)
    cosine, sine_table = rope_tables(positions)

    def rope_pair(query_part, key_part):
        return (
            rotate(query_part.reshape(row_count, HEADS, HEAD_DIM), cosine, sine_table),
            rotate(key_part.reshape(row_count, KV_HEADS, HEAD_DIM), cosine, sine_table),
        )

    (query_rot, key_rot), pull_rope = jax.vjp(
        rope_pair, projected[:, :q_width], projected[:, q_width : q_width + kv_width]
    )
    queries = query_rot.astype(jnp.bfloat16).reshape(row_count, KV_HEADS, group_size, HEAD_DIM)
    key_local = key_rot.reshape(row_count, kv_width).astype(jnp.bfloat16)
    value_local = projected[:, q_width + kv_width : offset_cols].astype(jnp.bfloat16)
    key_all, value_all = (
        lax.all_gather(key_local, "seq", axis=0, tiled=True),
        lax.all_gather(value_local, "seq", axis=0, tiled=True),
    )

    def scores_for(key_source, shard):
        key_block = lax.dynamic_slice_in_dim(key_source, shard * row_count, row_count, 0)
        key_block = key_block.reshape(row_count, KV_HEADS, HEAD_DIM)
        raw_scores = (
            jnp.einsum("qkgd,skd->kgqs", queries, key_block, preferred_element_type=jnp.float32)
            * scale_factor
        )
        key_pos = shard * row_count + jnp.arange(row_count, dtype=jnp.int32)
        allowed = key_pos[None, :] <= positions[:, None]
        return jnp.where(allowed, raw_scores, -1e30)

    def value_block(value_source, shard):
        picked = lax.dynamic_slice_in_dim(value_source, shard * row_count, row_count, 0)
        return picked.reshape(row_count, KV_HEADS, HEAD_DIM)

    def max_step(shard, carry):
        row_top, row_total = carry
        scores = scores_for(key_all, shard)
        new_top = jnp.maximum(row_top, jnp.max(scores, axis=-1))
        row_total = row_total * jnp.exp(row_top - new_top) + jnp.sum(
            jnp.exp(scores - new_top[..., None]), axis=-1
        )
        return (new_top, row_total)

    start_top = jnp.full((KV_HEADS, group_size, row_count), -1e30, jnp.float32)
    row_top, row_total = lax.fori_loop(
        0, seq_index + 1, max_step, (start_top, jnp.zeros_like(start_top))
    )
    log_total = row_top + jnp.log(row_total)

    def out_step(shard, accum):
        scores = scores_for(key_all, shard)
        probability = jnp.exp(scores - log_total[..., None]).astype(jnp.bfloat16)
        return accum + jnp.einsum(
            "kgqs,skd->qkgd",
            probability,
            value_block(value_all, shard),
            preferred_element_type=jnp.float32,
        )

    attended_f = lax.fori_loop(
        0,
        seq_index + 1,
        out_step,
        jnp.zeros((row_count, KV_HEADS, group_size, HEAD_DIM), jnp.float32),
    )
    attended = (attended_f * out_multiplier).reshape(row_count, q_width).astype(jnp.bfloat16)
    gate_z = projected[:, offset_cols : offset_cols + inner_width]
    xbc_raw = projected[:, offset_cols + inner_width : offset_cols + inner_width + conv_width]
    dt_raw = projected[:, offset_cols + inner_width + conv_width :]
    rim_rows = from_behind(xbc_raw[row_count - (CONV - 1) :], "seq", 1)
    padded = jnp.concatenate([rim_rows, xbc_raw], axis=0)
    (inputs, log_decay, b_matrix, c_matrix, x_heads), pull_prep = jax.vjp(
        prepare, padded, conv_taps, head_params, dt_raw
    )
    (decay_all, end_state), pull_state = jax.vjp(local_state, inputs, log_decay, b_matrix)
    decay_identity = jnp.ones_like(decay_all)
    state_identity = jnp.zeros_like(end_state)
    before_decay, start_state = entering(
        (decay_all, end_state), "seq", chain_step, (decay_identity, state_identity)
    )
    mamba_f, pull_out = jax.vjp(
        mamba_output,
        inputs,
        log_decay,
        b_matrix,
        c_matrix,
        x_heads,
        gate_z,
        head_params,
        gain_mamba,
        start_state,
    )
    joined = jnp.concatenate([attended, mamba_f.astype(jnp.bfloat16)], axis=1)
    hidden = tokens_f + jnp.dot(joined, full_mixout, preferred_element_type=jnp.float32)
    normed2_f, pull_second = jax.vjp(rms_scale, hidden, gain_second)
    normed2 = normed2_f.astype(jnp.bfloat16)
    gate_up = jnp.dot(normed2, full_gateup, preferred_element_type=jnp.float32)
    swiglu_out, pull_swiglu = jax.vjp(swiglu, gate_up)
    activated = swiglu_out.astype(jnp.bfloat16)
    out_block = (hidden + jnp.dot(activated, full_down, preferred_element_type=jnp.float32)).astype(
        jnp.bfloat16
    )
    back_project, back_mixout, back_gateup, back_down = (
        full_project,
        full_mixout,
        full_gateup,
        full_down,
    )
    grad_out = cotangent.astype(jnp.float32)
    grad_down = jnp.einsum("tf,td->fd", activated, cotangent, preferred_element_type=jnp.float32)
    grad_act = jnp.einsum("td,fd->tf", cotangent, back_down, preferred_element_type=jnp.float32)
    (grad_gu_f,) = pull_swiglu(grad_act)
    grad_gu = grad_gu_f.astype(jnp.bfloat16)
    grad_gateup = jnp.einsum("tc,tf->cf", normed2, grad_gu, preferred_element_type=jnp.float32)
    grad_normed2 = jnp.einsum("tf,cf->tc", grad_gu, back_gateup, preferred_element_type=jnp.float32)
    grad_hidden_n, grad_gain_second = pull_second(grad_normed2)
    grad_hidden = grad_out + grad_hidden_n
    grad_branch = grad_hidden.astype(jnp.bfloat16)
    grad_mixout = jnp.einsum("tr,td->rd", joined, grad_branch, preferred_element_type=jnp.float32)
    pair = jnp.stack([grad_mixout, grad_down], axis=0).astype(jnp.bfloat16)
    pair = jnp.transpose(pair.reshape(2, devices, 2, share, D), (1, 3, 2, 0, 4))
    early = jnp.concatenate(
        [grad_gateup.astype(jnp.bfloat16), pair.reshape(devices * share, 4 * D)], axis=1
    )
    early, grad_branch = lax.optimization_barrier((early, grad_branch))
    own_early = lax.psum_scatter(early, ("batch", "seq"), scatter_dimension=0, tiled=True)
    grad_joined = jnp.einsum(
        "td,rd->tr", grad_branch, back_mixout, preferred_element_type=jnp.float32
    )
    grad_att = (
        grad_joined[:, :q_width]
        .astype(jnp.bfloat16)
        .reshape(row_count, KV_HEADS, group_size, HEAD_DIM)
    )
    grad_mamba = grad_joined[:, q_width:]
    key_back, value_back = (key_all, value_all)
    delta_rows = out_multiplier * jnp.transpose(
        jnp.sum(grad_att.astype(jnp.float32) * attended_f, axis=-1), (1, 2, 0)
    )

    def back_step(shard, carry):
        grad_query, grad_kv = carry
        scores = scores_for(key_back, shard)
        probability = jnp.exp(scores - log_total[..., None])
        value_rows = value_block(value_back, shard)
        key_rows = value_block(key_back, shard)
        grad_probs = out_multiplier * jnp.einsum(
            "qkgd,skd->kgqs", grad_att, value_rows, preferred_element_type=jnp.float32
        )
        grad_scores = (probability * (grad_probs - delta_rows[..., None])).astype(jnp.bfloat16)
        grad_query = grad_query + scale_factor * jnp.einsum(
            "kgqs,skd->qkgd", grad_scores, key_rows, preferred_element_type=jnp.float32
        )
        grad_keys = scale_factor * jnp.einsum(
            "kgqs,qkgd->skd", grad_scores, queries, preferred_element_type=jnp.float32
        )
        grad_values = out_multiplier * jnp.einsum(
            "kgqs,qkgd->skd",
            probability.astype(jnp.bfloat16),
            grad_att,
            preferred_element_type=jnp.float32,
        )
        block_rows = jnp.concatenate(
            [grad_keys.reshape(row_count, kv_width), grad_values.reshape(row_count, kv_width)],
            axis=1,
        )
        grad_kv = lax.dynamic_update_slice_in_dim(grad_kv, block_rows, shard * row_count, 0)
        return (grad_query, grad_kv)

    length_rows = key_back.shape[0]
    grad_query, grad_kv = lax.fori_loop(
        0,
        seq_index + 1,
        back_step,
        (
            jnp.zeros((row_count, KV_HEADS, group_size, HEAD_DIM), jnp.float32),
            jnp.zeros((length_rows, 2 * kv_width), jnp.float32),
        ),
    )
    grad_kv_own = lax.psum_scatter(
        grad_kv.astype(jnp.bfloat16), "seq", scatter_dimension=0, tiled=True
    ).astype(jnp.float32)
    grad_query_pre, grad_key_pre = pull_rope(
        (
            grad_query.reshape(row_count, HEADS, HEAD_DIM),
            grad_kv_own[:, :kv_width].reshape(row_count, KV_HEADS, HEAD_DIM),
        )
    )
    g_inputs, g_logd, g_bmat, g_cmat, g_xheads, g_gate_z, g_head_out, g_gain_mamba, g_start = (
        pull_out(grad_mamba)
    )
    later_decay, carry_grad = entering_2(
        (decay_all, g_start), "seq", chain_step, (decay_identity, state_identity)
    )
    g_decay = jnp.sum(carry_grad * start_state, axis=(1, 2))
    g_inputs_end, g_logd_end, g_bmat_end = pull_state((g_decay, carry_grad))
    g_padded, g_conv, g_head_prep, g_dtraw = pull_prep(
        (g_inputs + g_inputs_end, g_logd + g_logd_end, g_bmat + g_bmat_end, g_cmat, g_xheads)
    )
    back_rim = from_behind(g_padded[: CONV - 1], "seq", -1)
    g_xbc = g_padded[CONV - 1 :]
    g_xbc = jnp.concatenate(
        [g_xbc[: row_count - (CONV - 1)], g_xbc[row_count - (CONV - 1) :] + back_rim], axis=0
    )
    grad_projected = jnp.concatenate(
        [grad_query_pre, grad_key_pre, grad_kv_own[:, kv_width:], g_gate_z, g_xbc, g_dtraw], axis=1
    ).astype(jnp.bfloat16)
    grad_project = jnp.einsum(
        "tc,tk->ck", normed, grad_projected, preferred_element_type=jnp.float32
    )
    grad_normed = jnp.einsum(
        "tk,ck->tc", grad_projected, back_project, preferred_element_type=jnp.float32
    )
    grad_tokens_n, grad_gain_first = pull_first(grad_normed)
    grad_tokens = grad_hidden + grad_tokens_n
    grad_gains = jnp.concatenate([grad_gain_first, grad_gain_second, g_gain_mamba], axis=0)
    late = pack_late(grad_project, grad_gains, g_conv, devices)
    own_late = lax.psum_scatter(late, ("batch", "seq"), scatter_dimension=0, tiled=True).astype(
        jnp.float32
    )
    own_project = own_late[:, : w_project.shape[1]]
    own_gains, own_conv = unpack_vectors(own_late, w_project.shape[1], 1, gains, conv_params)
    grad_head = lax.psum(g_head_out + g_head_prep, ("batch", "seq"))
    own_early = own_early.astype(jnp.float32)
    own_gateup = own_early[:, : 2 * FF]
    own_pair = own_early[:, 2 * FF :].reshape(share, 2, 2, D)
    own_pair = jnp.transpose(own_pair, (2, 1, 0, 3)).reshape(2, 2 * share, D)
    own_mixout, own_down = own_pair[0], own_pair[1]
    r_project = adamw_update(
        w_project, own_project, mom_project, sec_project, rate_matrix, weight_decay
    )
    r_mixout = adamw_update(w_mixout, own_mixout, mom_mixout, sec_mixout, rate_matrix, weight_decay)
    r_gateup = adamw_update(w_gateup, own_gateup, mom_gateup, sec_gateup, rate_matrix, weight_decay)
    r_down = adamw_update(w_down, own_down, mom_down, sec_down, rate_matrix, weight_decay)
    r_gains = adamw_update(gains, own_gains, mom_gains, sec_gains, rate_vector, 0.0)
    r_conv = adamw_update(conv_params, own_conv, mom_conv, sec_conv, rate_vector, 0.0)
    r_head = adamw_update(head_params, grad_head, mom_head, sec_head, rate_vector, 0.0)
    return (
        out_block,
        grad_tokens,
        r_project[0],
        r_project[1],
        r_project[2],
        r_mixout[0],
        r_mixout[1],
        r_mixout[2],
        r_gateup[0],
        r_gateup[1],
        r_gateup[2],
        r_down[0],
        r_down[1],
        r_down[2],
        r_gains[0],
        r_gains[1],
        r_gains[2],
        r_conv[0],
        r_conv[1],
        r_conv[2],
        r_head[0],
        r_head[1],
        r_head[2],
    )


def solution(mesh):
    return jax.shard_map(
        local,
        mesh=mesh,
        in_specs=(
            P(("batch", "seq"), None),
            P(("batch", "seq"), None),
            P(("batch", "seq"), None),
            P(("batch", "seq"), None),
            P(("batch", "seq"), None),
            P(("batch", "seq"), None),
            P(("batch", "seq")),
            P(None, ("batch", "seq")),
            P(),
            P(("batch", "seq"), None),
            P(("batch", "seq"), None),
            P(("batch", "seq"), None),
            P(("batch", "seq"), None),
            P(("batch", "seq"), None),
            P(("batch", "seq"), None),
            P(("batch", "seq"), None),
            P(("batch", "seq"), None),
            P(("batch", "seq")),
            P(("batch", "seq")),
            P(None, ("batch", "seq")),
            P(None, ("batch", "seq")),
            P(),
            P(),
        ),
        out_specs=(
            P(("batch", "seq"), None),
            P(("batch", "seq"), None),
            P(("batch", "seq"), None),
            P(("batch", "seq"), None),
            P(("batch", "seq"), None),
            P(("batch", "seq"), None),
            P(("batch", "seq"), None),
            P(("batch", "seq"), None),
            P(("batch", "seq"), None),
            P(("batch", "seq"), None),
            P(("batch", "seq"), None),
            P(("batch", "seq"), None),
            P(("batch", "seq"), None),
            P(("batch", "seq"), None),
            P(("batch", "seq")),
            P(("batch", "seq")),
            P(("batch", "seq")),
            P(None, ("batch", "seq")),
            P(None, ("batch", "seq")),
            P(None, ("batch", "seq")),
            P(),
            P(),
            P(),
        ),
        check_vma=False,
    )
```

```python
import jax
import jax.numpy as jnp
from jax import lax
from jax.sharding import PartitionSpec as P

D = 1024
FF = 2048
HEADS = 8
KV_HEADS = 2
HEAD_DIM = 64
M_HEADS = 24
M_DIM = 64
STATE = 128
CONV = 4
STEP = 10


epsilon = 1e-05
rope_base = 100000000000.0
beta_one = 0.9
beta_two = 0.95
adam_eps = 1e-08
weight_decay = 0.1
rate_matrix = 0.06
rate_vector = 1.0
highest = lax.Precision.HIGHEST


def from_behind(value, axis, by):
    length = lax.axis_size(axis)
    pairs = [(i, i + by) for i in range(length) if 0 <= i + by < length]
    return lax.ppermute(value, axis, pairs)


def entering(value, axis, join, neutral):
    place = lax.axis_index(axis)
    gathered = jax.tree.map(
        lambda a, kind: lax.all_gather(a.astype(kind), axis), value, (jnp.bfloat16, jnp.bfloat16)
    )
    state = jax.tree.map(lambda a, e: jnp.zeros_like(a) + jnp.asarray(e, a.dtype), value, neutral)

    def one(turn, state):
        return join(
            state,
            jax.tree.map(
                lambda a, own: lax.dynamic_index_in_dim(a, turn, 0, False).astype(own.dtype),
                gathered,
                value,
            ),
        )

    return lax.fori_loop(0, place, one, state)


def entering_2(value, axis, combine, identity):
    length, index = (lax.axis_size(axis), lax.axis_index(axis))
    everything = jax.tree.map(
        lambda part, kind: lax.all_gather(part.astype(kind), axis),
        value,
        jax.tree.map(lambda a: jnp.bfloat16 if a.dtype == jnp.float32 else a.dtype, value),
    )
    start = jax.tree.map(
        lambda part, zero: jnp.broadcast_to(jnp.asarray(zero, part.dtype), part.shape),
        value,
        identity,
    )

    def turn(k, before):
        at = length - 1 - k
        reached = at > index
        new = combine(
            before, jax.tree.map(lambda part, own: part[at].astype(own.dtype), everything, value)
        )
        return jax.tree.map(lambda a, b: jnp.where(reached, a, b), new, before)

    return lax.fori_loop(0, length, turn, start)


def hp_matmul(left, right):
    return jnp.dot(left, right, precision=highest, preferred_element_type=jnp.float32)


def rms_scale(values, gain_vector):
    return (
        values
        * lax.rsqrt(jnp.mean(values * values, axis=-1, keepdims=True) + epsilon)
        * gain_vector
    )


def rope_tables(positions):
    half_dim = HEAD_DIM // 2
    frequency = jnp.power(rope_base, -2.0 * jnp.arange(half_dim, dtype=jnp.float32) / HEAD_DIM)
    angles = positions.astype(jnp.float32)[:, None] * frequency[None, :]
    return (jnp.cos(angles)[:, None, :], jnp.sin(angles)[:, None, :])


def rotate(heads, cosine, sine_table):
    half_dim = HEAD_DIM // 2
    first_half = heads[..., :half_dim]
    second_half = heads[..., half_dim:]
    return jnp.concatenate(
        [
            first_half * cosine - second_half * sine_table,
            second_half * cosine + first_half * sine_table,
        ],
        axis=-1,
    )


def prepare(padded, conv_taps, head_params, dt_raw):
    row_count = dt_raw.shape[0]
    inner_width = M_HEADS * M_DIM
    summed = conv_taps[CONV]
    for tap_index in range(CONV):
        summed = summed + conv_taps[tap_index] * padded[tap_index : tap_index + row_count]
    activated = jax.nn.silu(summed)
    x_heads = activated[:, :inner_width].reshape(row_count, M_HEADS, M_DIM)
    b_matrix = activated[:, inner_width : inner_width + STATE]
    c_matrix = activated[:, inner_width + STATE :]
    step_size = jax.nn.softplus(dt_raw + head_params[0])
    log_decay = -step_size * jnp.exp(head_params[1])
    return (step_size[:, :, None] * x_heads, log_decay, b_matrix, c_matrix, x_heads)


def local_state(inputs, log_decay, b_matrix):
    cumulated = jnp.cumsum(log_decay, axis=0)
    tail_decay = jnp.exp(cumulated[-1][None, :] - cumulated)
    end_state = jnp.einsum(
        "shp,sn->hpn", tail_decay[:, :, None] * inputs, b_matrix, precision=highest
    )
    return (jnp.exp(cumulated[-1]), end_state)


def mamba_output(
    inputs, log_decay, b_matrix, c_matrix, x_heads, gate_z, head_params, gain_vector, start_state
):
    row_count = log_decay.shape[0]
    cumulated = jnp.cumsum(log_decay, axis=0)
    lower_mask = (jnp.arange(row_count)[:, None] >= jnp.arange(row_count)[None, :])[:, :, None]
    log_gaps = jnp.where(lower_mask, cumulated[:, None, :] - cumulated[None, :, :], -1e30)
    mixing = hp_matmul(c_matrix, b_matrix.T)[:, :, None] * jnp.exp(log_gaps)
    within = jnp.einsum("tsh,shp->thp", mixing, inputs, precision=highest)
    carried = (
        jnp.einsum("tn,hpn->thp", c_matrix, start_state, precision=highest)
        * jnp.exp(cumulated)[:, :, None]
    )
    output = within + carried + head_params[2][None, :, None] * x_heads
    gated = output.reshape(row_count, M_HEADS * M_DIM) * jax.nn.silu(gate_z)
    return rms_scale(gated, gain_vector)


def chain_step(earlier, later):
    return (earlier[0] * later[0], later[0][:, None, None] * earlier[1] + later[1])


def swiglu(gate_part, up_part):
    return jax.nn.silu(gate_part) * up_part


def index_bits():
    found = []
    for axis in ("seq", "batch"):
        found += [(axis, 1 << k) for k in range(lax.axis_size(axis).bit_length() - 1)]
    return found


def exchange_orders(bits):
    along = [bit for bit in bits if bit[0] == "seq"]
    across = [bit for bit in bits if bit[0] == "batch"]
    core, xs = along[:1], along[1:]
    ys, zs, last = across[:-2], across[-2:-1], across[-1:]
    return core + xs + ys + zs + last, core + ys + zs + xs + last, core + zs + xs + ys + last


def swapped(value, bit):
    axis, mask = bit
    pairs = [(i, i ^ mask) for i in range(lax.axis_size(axis))]
    return lax.ppermute(value, axis, pairs)


def own_bit(bit):
    axis, mask = bit
    return (lax.axis_index(axis) // mask) % 2


def gather_rows(block, bits, order):
    rows, width = block.shape
    held = []
    for bit in reversed(order):
        other = swapped(block, bit)
        below = sum(1 for b in held if bits.index(b) < bits.index(bit))
        split = ((1 << (len(held) - below)), (1 << below) * rows, width)
        mine, theirs = block.reshape(split), other.reshape(split)
        low = own_bit(bit) == 0
        block = jnp.stack(
            [jnp.where(low, mine, theirs), jnp.where(low, theirs, mine)], axis=1
        ).reshape(-1, width)
        held.append(bit)
    return block


def scatter_rows(total, bits, order):
    rows, width = total.shape[0] >> len(bits), total.shape[1]
    left = list(bits)
    for bit in order:
        below = left.index(bit)
        left.remove(bit)
        split = total.reshape(1 << (len(left) - below), 2, (1 << below) * rows, width)
        place = own_bit(bit)
        keep = lax.dynamic_index_in_dim(split, place, 1, False).reshape(-1, width)
        send = lax.dynamic_index_in_dim(split, 1 - place, 1, False).reshape(-1, width)
        got = swapped(send, bit)
        total = (keep.astype(jnp.float32) + got.astype(jnp.float32)).astype(total.dtype)
    return total


def sum_everywhere(value, bits):
    for bit in bits:
        value = value + swapped(value, bit)
    return value


def adamw_update(weight, gradient, moment_one, moment_two, rate, decay):
    moment_one = beta_one * moment_one + (1.0 - beta_one) * gradient
    moment_two = beta_two * moment_two + (1.0 - beta_two) * gradient * gradient
    corrected_one = moment_one / (1.0 - beta_one**STEP)
    corrected_two = moment_two / (1.0 - beta_two**STEP)
    new_weight = weight - rate * (
        corrected_one / (jnp.sqrt(corrected_two) + adam_eps) + decay * weight
    )
    return (moment_one, moment_two, new_weight)


def pack_project(weights, gains, taps):
    rows = weights.shape[0]
    vectors = jnp.concatenate([gains, taps.reshape(-1)])
    width = -(-vectors.shape[0] // rows)
    vectors = jnp.pad(vectors, (0, width * rows - vectors.shape[0])).reshape(rows, width)
    return jnp.concatenate([weights, vectors], axis=1).astype(jnp.bfloat16)


def unpack_vectors(packed, start, devices, gains, taps):
    vectors = packed[:, start:].reshape(devices, -1)
    count = gains.shape[0]
    own_gains = vectors[:, :count].reshape(-1)
    own_taps = vectors[:, count : count + taps.size].reshape(devices, CONV + 1, taps.shape[1])
    return own_gains, jnp.transpose(own_taps, (1, 0, 2)).reshape(CONV + 1, -1)


def local(
    tokens,
    cotangent,
    w_project,
    w_mixout,
    w_gateup,
    w_down,
    gains,
    conv_params,
    head_params,
    mom_project,
    sec_project,
    mom_mixout,
    sec_mixout,
    mom_gateup,
    sec_gateup,
    mom_down,
    sec_down,
    mom_gains,
    sec_gains,
    mom_conv,
    sec_conv,
    mom_head,
    sec_head,
):
    row_count = tokens.shape[0]
    group_size = HEADS // KV_HEADS
    scale_factor = HEAD_DIM ** (-0.5)
    q_width = HEADS * HEAD_DIM
    kv_width = KV_HEADS * HEAD_DIM
    inner_width = M_HEADS * M_DIM
    conv_width = inner_width + 2 * STATE
    offset_cols = q_width + 2 * kv_width
    out_multiplier = (row_count * lax.axis_size("seq") / 6.0) ** 0.5
    devices = lax.axis_size("batch") * lax.axis_size("seq")
    share = w_project.shape[0]
    full_packed = lax.all_gather(
        pack_project(w_project, gains, conv_params), ("batch", "seq"), axis=0, tiled=True
    )
    full_project = full_packed[:, : w_project.shape[1]]
    full_gains, full_conv = unpack_vectors(full_packed, w_project.shape[1], devices, gains, conv_params)
    full_pair = lax.all_gather(
        jnp.concatenate([w_mixout, w_down], axis=0).astype(jnp.bfloat16),
        ("batch", "seq"),
        axis=0,
    )
    full_mixout = full_pair[:, : 2 * share].reshape(-1, D)
    full_down = full_pair[:, 2 * share :].reshape(-1, D)
    bits = index_bits()
    order_a, order_b, order_c = exchange_orders(bits)
    full_gate = gather_rows(w_gateup[:, :FF].astype(jnp.bfloat16), bits, order_a)
    full_up = gather_rows(w_gateup[:, FF:].astype(jnp.bfloat16), bits, order_b)
    gains_f = full_gains.astype(jnp.float32)
    gain_first = gains_f[:D]
    gain_second = gains_f[D : 2 * D]
    gain_mamba = gains_f[2 * D :]
    conv_taps = full_conv.astype(jnp.float32)
    tokens_f = tokens.astype(jnp.float32)
    normed_f, pull_first = jax.vjp(rms_scale, tokens_f, gain_first)
    normed = normed_f.astype(jnp.bfloat16)
    projected = jnp.dot(normed, full_project, preferred_element_type=jnp.float32)
    seq_index = lax.axis_index("seq")
    positions = seq_index * row_count + jnp.arange(row_count, dtype=jnp.int32)
    cosine, sine_table = rope_tables(positions)

    def rope_pair(query_part, key_part):
        return (
            rotate(query_part.reshape(row_count, HEADS, HEAD_DIM), cosine, sine_table),
            rotate(key_part.reshape(row_count, KV_HEADS, HEAD_DIM), cosine, sine_table),
        )

    (query_rot, key_rot), pull_rope = jax.vjp(
        rope_pair, projected[:, :q_width], projected[:, q_width : q_width + kv_width]
    )
    queries = query_rot.astype(jnp.bfloat16).reshape(row_count, KV_HEADS, group_size, HEAD_DIM)
    key_local = key_rot.reshape(row_count, kv_width).astype(jnp.bfloat16)
    value_local = projected[:, q_width + kv_width : offset_cols].astype(jnp.bfloat16)
    key_value = lax.all_gather(
        jnp.concatenate([key_local, value_local], axis=1), "seq", axis=0, tiled=True
    )
    key_all, value_all = key_value[:, :kv_width], key_value[:, kv_width:]

    def scores_for(key_source, shard):
        key_block = lax.dynamic_slice_in_dim(key_source, shard * row_count, row_count, 0)
        key_block = key_block.reshape(row_count, KV_HEADS, HEAD_DIM)
        raw_scores = (
            jnp.einsum("qkgd,skd->kgqs", queries, key_block, preferred_element_type=jnp.float32)
            * scale_factor
        )
        key_pos = shard * row_count + jnp.arange(row_count, dtype=jnp.int32)
        allowed = key_pos[None, :] <= positions[:, None]
        return jnp.where(allowed, raw_scores, -1e30)

    def value_block(value_source, shard):
        picked = lax.dynamic_slice_in_dim(value_source, shard * row_count, row_count, 0)
        return picked.reshape(row_count, KV_HEADS, HEAD_DIM)

    def max_step(shard, carry):
        row_top, row_total = carry
        scores = scores_for(key_all, shard)
        new_top = jnp.maximum(row_top, jnp.max(scores, axis=-1))
        row_total = row_total * jnp.exp(row_top - new_top) + jnp.sum(
            jnp.exp(scores - new_top[..., None]), axis=-1
        )
        return (new_top, row_total)

    start_top = jnp.full((KV_HEADS, group_size, row_count), -1e30, jnp.float32)
    row_top, row_total = lax.fori_loop(
        0, seq_index + 1, max_step, (start_top, jnp.zeros_like(start_top))
    )
    log_total = row_top + jnp.log(row_total)

    def out_step(shard, accum):
        scores = scores_for(key_all, shard)
        probability = jnp.exp(scores - log_total[..., None]).astype(jnp.bfloat16)
        return accum + jnp.einsum(
            "kgqs,skd->qkgd",
            probability,
            value_block(value_all, shard),
            preferred_element_type=jnp.float32,
        )

    attended_f = lax.fori_loop(
        0,
        seq_index + 1,
        out_step,
        jnp.zeros((row_count, KV_HEADS, group_size, HEAD_DIM), jnp.float32),
    )
    attended = (attended_f * out_multiplier).reshape(row_count, q_width).astype(jnp.bfloat16)
    gate_z = projected[:, offset_cols : offset_cols + inner_width]
    xbc_raw = projected[:, offset_cols + inner_width : offset_cols + inner_width + conv_width]
    dt_raw = projected[:, offset_cols + inner_width + conv_width :]
    rim_rows = from_behind(xbc_raw[row_count - (CONV - 1) :], "seq", 1)
    padded = jnp.concatenate([rim_rows, xbc_raw], axis=0)
    (inputs, log_decay, b_matrix, c_matrix, x_heads), pull_prep = jax.vjp(
        prepare, padded, conv_taps, head_params, dt_raw
    )
    (decay_all, end_state), pull_state = jax.vjp(local_state, inputs, log_decay, b_matrix)
    decay_identity = jnp.ones_like(decay_all)
    state_identity = jnp.zeros_like(end_state)
    before_decay, start_state = entering(
        (decay_all, end_state), "seq", chain_step, (decay_identity, state_identity)
    )
    mamba_f, pull_out = jax.vjp(
        mamba_output,
        inputs,
        log_decay,
        b_matrix,
        c_matrix,
        x_heads,
        gate_z,
        head_params,
        gain_mamba,
        start_state,
    )
    joined = jnp.concatenate([attended, mamba_f.astype(jnp.bfloat16)], axis=1)
    hidden = tokens_f + jnp.dot(joined, full_mixout, preferred_element_type=jnp.float32)
    normed2_f, pull_second = jax.vjp(rms_scale, hidden, gain_second)
    normed2 = normed2_f.astype(jnp.bfloat16)
    gate_part = jnp.dot(normed2, full_gate, preferred_element_type=jnp.float32)
    up_part = jnp.dot(normed2, full_up, preferred_element_type=jnp.float32)
    swiglu_out, pull_swiglu = jax.vjp(swiglu, gate_part, up_part)
    activated = swiglu_out.astype(jnp.bfloat16)
    out_block = (hidden + jnp.dot(activated, full_down, preferred_element_type=jnp.float32)).astype(
        jnp.bfloat16
    )
    back_project, back_mixout, back_down = (
        full_project,
        full_mixout,
        full_down,
    )
    grad_out = cotangent.astype(jnp.float32)
    grad_down = jnp.einsum("tf,td->fd", activated, cotangent, preferred_element_type=jnp.float32)
    grad_act = jnp.einsum("td,fd->tf", cotangent, back_down, preferred_element_type=jnp.float32)
    grad_gate_f, grad_up_f = pull_swiglu(grad_act)
    grad_gate_t = grad_gate_f.astype(jnp.bfloat16)
    grad_up_t = grad_up_f.astype(jnp.bfloat16)
    grad_gate = jnp.einsum("tc,tf->cf", normed2, grad_gate_t, preferred_element_type=jnp.float32)
    grad_up = jnp.einsum("tc,tf->cf", normed2, grad_up_t, preferred_element_type=jnp.float32)
    grad_normed2 = jnp.einsum(
        "tf,cf->tc", grad_gate_t, full_gate, preferred_element_type=jnp.float32
    ) + jnp.einsum("tf,cf->tc", grad_up_t, full_up, preferred_element_type=jnp.float32)
    grad_hidden_n, grad_gain_second = pull_second(grad_normed2)
    grad_hidden = grad_out + grad_hidden_n
    grad_branch = grad_hidden.astype(jnp.bfloat16)
    grad_mixout = jnp.einsum("tr,td->rd", joined, grad_branch, preferred_element_type=jnp.float32)
    early = tuple(g.astype(jnp.bfloat16) for g in (grad_down, grad_mixout, grad_gate, grad_up))
    early, grad_branch = lax.optimization_barrier((early, grad_branch))
    own_down = scatter_rows(early[0], bits, order_a).astype(jnp.float32)
    own_mixout = scatter_rows(early[1], bits, order_b).astype(jnp.float32)
    own_gate = scatter_rows(early[2], bits, order_c).astype(jnp.float32)
    own_up = scatter_rows(early[3], bits, order_a).astype(jnp.float32)
    own_gateup = jnp.concatenate([own_gate, own_up], axis=1)
    grad_joined = jnp.einsum(
        "td,rd->tr", grad_branch, back_mixout, preferred_element_type=jnp.float32
    )
    grad_att = (
        grad_joined[:, :q_width]
        .astype(jnp.bfloat16)
        .reshape(row_count, KV_HEADS, group_size, HEAD_DIM)
    )
    grad_mamba = grad_joined[:, q_width:]
    key_back, value_back = (key_all, value_all)
    delta_rows = out_multiplier * jnp.transpose(
        jnp.sum(grad_att.astype(jnp.float32) * attended_f, axis=-1), (1, 2, 0)
    )

    def back_step(shard, carry):
        grad_query, grad_kv = carry
        scores = scores_for(key_back, shard)
        probability = jnp.exp(scores - log_total[..., None])
        value_rows = value_block(value_back, shard)
        key_rows = value_block(key_back, shard)
        grad_probs = out_multiplier * jnp.einsum(
            "qkgd,skd->kgqs", grad_att, value_rows, preferred_element_type=jnp.float32
        )
        grad_scores = (probability * (grad_probs - delta_rows[..., None])).astype(jnp.bfloat16)
        grad_query = grad_query + scale_factor * jnp.einsum(
            "kgqs,skd->qkgd", grad_scores, key_rows, preferred_element_type=jnp.float32
        )
        grad_keys = scale_factor * jnp.einsum(
            "kgqs,qkgd->skd", grad_scores, queries, preferred_element_type=jnp.float32
        )
        grad_values = out_multiplier * jnp.einsum(
            "kgqs,qkgd->skd",
            probability.astype(jnp.bfloat16),
            grad_att,
            preferred_element_type=jnp.float32,
        )
        block_rows = jnp.concatenate(
            [grad_keys.reshape(row_count, kv_width), grad_values.reshape(row_count, kv_width)],
            axis=1,
        )
        grad_kv = lax.dynamic_update_slice_in_dim(grad_kv, block_rows, shard * row_count, 0)
        return (grad_query, grad_kv)

    length_rows = key_back.shape[0]
    grad_query, grad_kv = lax.fori_loop(
        0,
        seq_index + 1,
        back_step,
        (
            jnp.zeros((row_count, KV_HEADS, group_size, HEAD_DIM), jnp.float32),
            jnp.zeros((length_rows, 2 * kv_width), jnp.float32),
        ),
    )
    grad_kv_own = lax.psum_scatter(
        grad_kv.astype(jnp.bfloat16), "seq", scatter_dimension=0, tiled=True
    ).astype(jnp.float32)
    grad_query_pre, grad_key_pre = pull_rope(
        (
            grad_query.reshape(row_count, HEADS, HEAD_DIM),
            grad_kv_own[:, :kv_width].reshape(row_count, KV_HEADS, HEAD_DIM),
        )
    )
    g_inputs, g_logd, g_bmat, g_cmat, g_xheads, g_gate_z, g_head_out, g_gain_mamba, g_start = (
        pull_out(grad_mamba)
    )
    later_decay, carry_grad = entering_2(
        (decay_all, g_start), "seq", chain_step, (decay_identity, state_identity)
    )
    g_decay = jnp.sum(carry_grad * start_state, axis=(1, 2))
    g_inputs_end, g_logd_end, g_bmat_end = pull_state((g_decay, carry_grad))
    g_padded, g_conv, g_head_prep, g_dtraw = pull_prep(
        (g_inputs + g_inputs_end, g_logd + g_logd_end, g_bmat + g_bmat_end, g_cmat, g_xheads)
    )
    back_rim = from_behind(g_padded[: CONV - 1], "seq", -1)
    g_xbc = g_padded[CONV - 1 :]
    g_xbc = jnp.concatenate(
        [g_xbc[: row_count - (CONV - 1)], g_xbc[row_count - (CONV - 1) :] + back_rim], axis=0
    )
    grad_projected = jnp.concatenate(
        [grad_query_pre, grad_key_pre, grad_kv_own[:, kv_width:], g_gate_z, g_xbc, g_dtraw], axis=1
    ).astype(jnp.bfloat16)
    half_cols = offset_cols + inner_width
    grad_project = jnp.einsum(
        "tc,tk->ck", normed, grad_projected, preferred_element_type=jnp.float32
    ).astype(jnp.bfloat16)
    grad_left, grad_right = grad_project[:, :half_cols], grad_project[:, half_cols:]
    grad_normed = jnp.einsum(
        "tk,ck->tc", grad_projected, back_project, preferred_element_type=jnp.float32
    )
    grad_tokens_n, grad_gain_first = pull_first(grad_normed)
    grad_tokens = grad_hidden + grad_tokens_n
    grad_gains = jnp.concatenate([grad_gain_first, grad_gain_second, g_gain_mamba], axis=0)
    own_left = scatter_rows(grad_left.astype(jnp.bfloat16), bits, order_b)
    own_right = scatter_rows(grad_right.astype(jnp.bfloat16), bits, order_c)
    own_project = jnp.concatenate([own_left, own_right], axis=1).astype(jnp.float32)
    head_part = g_head_out + g_head_prep
    vectors = jnp.concatenate([grad_gains, g_conv.reshape(-1), head_part.reshape(-1)])
    vectors = jnp.pad(vectors, (0, -vectors.shape[0] % 1024)).reshape(-1, 128)
    vectors = sum_everywhere(vectors, bits).reshape(-1)
    place = lax.axis_index("batch") * lax.axis_size("seq") + lax.axis_index("seq")
    gain_count, tap_count = grad_gains.shape[0], g_conv.size
    own_gains = lax.dynamic_slice_in_dim(vectors, place * gains.shape[0], gains.shape[0])
    own_conv = lax.dynamic_slice_in_dim(
        vectors[gain_count : gain_count + tap_count].reshape(g_conv.shape),
        place * conv_params.shape[1],
        conv_params.shape[1],
        1,
    )
    grad_head = vectors[gain_count + tap_count : gain_count + tap_count + head_part.size]
    grad_head = grad_head.reshape(head_part.shape)
    r_project = adamw_update(
        w_project, own_project, mom_project, sec_project, rate_matrix, weight_decay
    )
    r_mixout = adamw_update(w_mixout, own_mixout, mom_mixout, sec_mixout, rate_matrix, weight_decay)
    r_gateup = adamw_update(w_gateup, own_gateup, mom_gateup, sec_gateup, rate_matrix, weight_decay)
    r_down = adamw_update(w_down, own_down, mom_down, sec_down, rate_matrix, weight_decay)
    r_gains = adamw_update(gains, own_gains, mom_gains, sec_gains, rate_vector, 0.0)
    r_conv = adamw_update(conv_params, own_conv, mom_conv, sec_conv, rate_vector, 0.0)
    r_head = adamw_update(head_params, grad_head, mom_head, sec_head, rate_vector, 0.0)
    return (
        out_block,
        grad_tokens,
        r_project[0],
        r_project[1],
        r_project[2],
        r_mixout[0],
        r_mixout[1],
        r_mixout[2],
        r_gateup[0],
        r_gateup[1],
        r_gateup[2],
        r_down[0],
        r_down[1],
        r_down[2],
        r_gains[0],
        r_gains[1],
        r_gains[2],
        r_conv[0],
        r_conv[1],
        r_conv[2],
        r_head[0],
        r_head[1],
        r_head[2],
    )


def solution(mesh):
    return jax.shard_map(
        local,
        mesh=mesh,
        in_specs=(
            P(("batch", "seq"), None),
            P(("batch", "seq"), None),
            P(("batch", "seq"), None),
            P(("batch", "seq"), None),
            P(("batch", "seq"), None),
            P(("batch", "seq"), None),
            P(("batch", "seq")),
            P(None, ("batch", "seq")),
            P(),
            P(("batch", "seq"), None),
            P(("batch", "seq"), None),
            P(("batch", "seq"), None),
            P(("batch", "seq"), None),
            P(("batch", "seq"), None),
            P(("batch", "seq"), None),
            P(("batch", "seq"), None),
            P(("batch", "seq"), None),
            P(("batch", "seq")),
            P(("batch", "seq")),
            P(None, ("batch", "seq")),
            P(None, ("batch", "seq")),
            P(),
            P(),
        ),
        out_specs=(
            P(("batch", "seq"), None),
            P(("batch", "seq"), None),
            P(("batch", "seq"), None),
            P(("batch", "seq"), None),
            P(("batch", "seq"), None),
            P(("batch", "seq"), None),
            P(("batch", "seq"), None),
            P(("batch", "seq"), None),
            P(("batch", "seq"), None),
            P(("batch", "seq"), None),
            P(("batch", "seq"), None),
            P(("batch", "seq"), None),
            P(("batch", "seq"), None),
            P(("batch", "seq"), None),
            P(("batch", "seq")),
            P(("batch", "seq")),
            P(("batch", "seq")),
            P(None, ("batch", "seq")),
            P(None, ("batch", "seq")),
            P(None, ("batch", "seq")),
            P(),
            P(),
            P(),
        ),
        check_vma=False,
    )
```

```python
import jax
import jax.numpy as jnp
from jax import lax
from jax.sharding import PartitionSpec as P

D = 1024
FF = 2048
HEADS = 8
KV_HEADS = 2
HEAD_DIM = 64
M_HEADS = 24
M_DIM = 64
STATE = 128
CONV = 4
STEP = 10


epsilon = 1e-05
rope_base = 100000000000.0
beta_one = 0.9
beta_two = 0.95
adam_eps = 1e-08
weight_decay = 0.1
rate_matrix = 0.06
rate_vector = 1.0
highest = lax.Precision.HIGHEST


def from_behind(value, axis, by):
    length = lax.axis_size(axis)
    pairs = [(i, i + by) for i in range(length) if 0 <= i + by < length]
    return lax.ppermute(value, axis, pairs)


def entering(value, axis, join, neutral):
    place = lax.axis_index(axis)
    gathered = jax.tree.map(
        lambda a, kind: lax.all_gather(a.astype(kind), axis), value, (jnp.bfloat16, jnp.bfloat16)
    )
    state = jax.tree.map(lambda a, e: jnp.zeros_like(a) + jnp.asarray(e, a.dtype), value, neutral)

    def one(turn, state):
        return join(
            state,
            jax.tree.map(
                lambda a, own: lax.dynamic_index_in_dim(a, turn, 0, False).astype(own.dtype),
                gathered,
                value,
            ),
        )

    return lax.fori_loop(0, place, one, state)


def entering_2(value, axis, combine, identity):
    length, index = (lax.axis_size(axis), lax.axis_index(axis))
    everything = jax.tree.map(
        lambda part, kind: lax.all_gather(part.astype(kind), axis),
        value,
        jax.tree.map(lambda a: jnp.bfloat16 if a.dtype == jnp.float32 else a.dtype, value),
    )
    start = jax.tree.map(
        lambda part, zero: jnp.broadcast_to(jnp.asarray(zero, part.dtype), part.shape),
        value,
        identity,
    )

    def turn(k, before):
        at = length - 1 - k
        reached = at > index
        new = combine(
            before, jax.tree.map(lambda part, own: part[at].astype(own.dtype), everything, value)
        )
        return jax.tree.map(lambda a, b: jnp.where(reached, a, b), new, before)

    return lax.fori_loop(0, length, turn, start)


def hp_matmul(left, right):
    return jnp.dot(left, right, precision=highest, preferred_element_type=jnp.float32)


def rms_scale(values, gain_vector):
    return (
        values
        * lax.rsqrt(jnp.mean(values * values, axis=-1, keepdims=True) + epsilon)
        * gain_vector
    )


def rope_tables(positions):
    half_dim = HEAD_DIM // 2
    frequency = jnp.power(rope_base, -2.0 * jnp.arange(half_dim, dtype=jnp.float32) / HEAD_DIM)
    angles = positions.astype(jnp.float32)[:, None] * frequency[None, :]
    return (jnp.cos(angles)[:, None, :], jnp.sin(angles)[:, None, :])


def rotate(heads, cosine, sine_table):
    half_dim = HEAD_DIM // 2
    first_half = heads[..., :half_dim]
    second_half = heads[..., half_dim:]
    return jnp.concatenate(
        [
            first_half * cosine - second_half * sine_table,
            second_half * cosine + first_half * sine_table,
        ],
        axis=-1,
    )


def prepare(padded, conv_taps, head_params, dt_raw):
    row_count = dt_raw.shape[0]
    inner_width = M_HEADS * M_DIM
    summed = conv_taps[CONV]
    for tap_index in range(CONV):
        summed = summed + conv_taps[tap_index] * padded[tap_index : tap_index + row_count]
    activated = jax.nn.silu(summed)
    x_heads = activated[:, :inner_width].reshape(row_count, M_HEADS, M_DIM)
    b_matrix = activated[:, inner_width : inner_width + STATE]
    c_matrix = activated[:, inner_width + STATE :]
    step_size = jax.nn.softplus(dt_raw + head_params[0])
    log_decay = -step_size * jnp.exp(head_params[1])
    return (step_size[:, :, None] * x_heads, log_decay, b_matrix, c_matrix, x_heads)


def local_state(inputs, log_decay, b_matrix):
    cumulated = jnp.cumsum(log_decay, axis=0)
    tail_decay = jnp.exp(cumulated[-1][None, :] - cumulated)
    end_state = jnp.einsum(
        "shp,sn->hpn", tail_decay[:, :, None] * inputs, b_matrix, precision=highest
    )
    return (jnp.exp(cumulated[-1]), end_state)


def mamba_output(
    inputs, log_decay, b_matrix, c_matrix, x_heads, gate_z, head_params, gain_vector, start_state
):
    row_count = log_decay.shape[0]
    cumulated = jnp.cumsum(log_decay, axis=0)
    lower_mask = (jnp.arange(row_count)[:, None] >= jnp.arange(row_count)[None, :])[:, :, None]
    log_gaps = jnp.where(lower_mask, cumulated[:, None, :] - cumulated[None, :, :], -1e30)
    mixing = hp_matmul(c_matrix, b_matrix.T)[:, :, None] * jnp.exp(log_gaps)
    within = jnp.einsum("tsh,shp->thp", mixing, inputs, precision=highest)
    carried = (
        jnp.einsum("tn,hpn->thp", c_matrix, start_state, precision=highest)
        * jnp.exp(cumulated)[:, :, None]
    )
    output = within + carried + head_params[2][None, :, None] * x_heads
    gated = output.reshape(row_count, M_HEADS * M_DIM) * jax.nn.silu(gate_z)
    return rms_scale(gated, gain_vector)


def chain_step(earlier, later):
    return (earlier[0] * later[0], later[0][:, None, None] * earlier[1] + later[1])


def swiglu(gate_part, up_part):
    return jax.nn.silu(gate_part) * up_part


def index_bits():
    found = []
    for axis in ("seq", "batch"):
        found += [(axis, 1 << k) for k in range(lax.axis_size(axis).bit_length() - 1)]
    return found


def exchange_orders(bits):
    along = [bit for bit in bits if bit[0] == "seq"]
    across = [bit for bit in bits if bit[0] == "batch"]
    core, xs = along[:1], along[1:]
    ys, zs, last = across[:-2], across[-2:-1], across[-1:]
    return core + xs + ys + zs + last, core + ys + zs + xs + last, core + zs + xs + ys + last


def swapped(value, bit):
    axis, mask = bit
    pairs = [(i, i ^ mask) for i in range(lax.axis_size(axis))]
    return lax.ppermute(value, axis, pairs)


def own_bit(bit):
    axis, mask = bit
    return (lax.axis_index(axis) // mask) % 2


def gather_rows(block, bits, order):
    rows, width = block.shape
    held = []
    for bit in reversed(order):
        other = swapped(block, bit)
        below = sum(1 for b in held if bits.index(b) < bits.index(bit))
        split = ((1 << (len(held) - below)), (1 << below) * rows, width)
        mine, theirs = block.reshape(split), other.reshape(split)
        low = own_bit(bit) == 0
        block = jnp.stack(
            [jnp.where(low, mine, theirs), jnp.where(low, theirs, mine)], axis=1
        ).reshape(-1, width)
        held.append(bit)
    return block


def scatter_rows(total, bits, order):
    rows, width = total.shape[0] >> len(bits), total.shape[1]
    left = list(bits)
    for bit in order:
        below = left.index(bit)
        left.remove(bit)
        split = total.reshape(1 << (len(left) - below), 2, (1 << below) * rows, width)
        place = own_bit(bit)
        keep = lax.dynamic_index_in_dim(split, place, 1, False).reshape(-1, width)
        send = lax.dynamic_index_in_dim(split, 1 - place, 1, False).reshape(-1, width)
        got = swapped(send, bit)
        total = (keep.astype(jnp.float32) + got.astype(jnp.float32)).astype(total.dtype)
    return total


def sum_everywhere(value, bits):
    for bit in bits:
        value = value + swapped(value, bit)
    return value


def adamw_update(weight, gradient, moment_one, moment_two, rate, decay):
    moment_one = beta_one * moment_one + (1.0 - beta_one) * gradient
    moment_two = beta_two * moment_two + (1.0 - beta_two) * gradient * gradient
    corrected_one = moment_one / (1.0 - beta_one**STEP)
    corrected_two = moment_two / (1.0 - beta_two**STEP)
    new_weight = weight - rate * (
        corrected_one / (jnp.sqrt(corrected_two) + adam_eps) + decay * weight
    )
    return (moment_one, moment_two, new_weight)


def pack_project(weights, gains, taps):
    rows = weights.shape[0]
    vectors = jnp.concatenate([gains, taps.reshape(-1)])
    width = -(-vectors.shape[0] // rows)
    vectors = jnp.pad(vectors, (0, width * rows - vectors.shape[0])).reshape(rows, width)
    return jnp.concatenate([weights, vectors], axis=1).astype(jnp.bfloat16)


def unpack_vectors(packed, start, devices, gains, taps):
    vectors = packed[:, start:].reshape(devices, -1)
    count = gains.shape[0]
    own_gains = vectors[:, :count].reshape(-1)
    own_taps = vectors[:, count : count + taps.size].reshape(devices, CONV + 1, taps.shape[1])
    return own_gains, jnp.transpose(own_taps, (1, 0, 2)).reshape(CONV + 1, -1)


def local(
    tokens,
    cotangent,
    w_project,
    w_mixout,
    w_gateup,
    w_down,
    gains,
    conv_params,
    head_params,
    mom_project,
    sec_project,
    mom_mixout,
    sec_mixout,
    mom_gateup,
    sec_gateup,
    mom_down,
    sec_down,
    mom_gains,
    sec_gains,
    mom_conv,
    sec_conv,
    mom_head,
    sec_head,
):
    row_count = tokens.shape[0]
    group_size = HEADS // KV_HEADS
    scale_factor = HEAD_DIM ** (-0.5)
    q_width = HEADS * HEAD_DIM
    kv_width = KV_HEADS * HEAD_DIM
    inner_width = M_HEADS * M_DIM
    conv_width = inner_width + 2 * STATE
    offset_cols = q_width + 2 * kv_width
    out_multiplier = (row_count * lax.axis_size("seq") / 6.0) ** 0.5
    devices = lax.axis_size("batch") * lax.axis_size("seq")
    share = w_project.shape[0]
    full_packed = lax.all_gather(
        pack_project(w_project, gains, conv_params), ("batch", "seq"), axis=0, tiled=True
    )
    pair = jnp.concatenate([w_mixout, w_down], axis=0).astype(jnp.bfloat16)
    pair, full_packed = lax.optimization_barrier((pair, full_packed))
    full_project = full_packed[:, : w_project.shape[1]]
    full_gains, full_conv = unpack_vectors(full_packed, w_project.shape[1], devices, gains, conv_params)
    full_pair = lax.all_gather(
        pair,
        ("batch", "seq"),
        axis=0,
    )
    full_mixout = full_pair[:, : 2 * share].reshape(-1, D)
    full_down = full_pair[:, 2 * share :].reshape(-1, D)
    bits = index_bits()
    order_a, order_b, order_c = exchange_orders(bits)
    full_gate = gather_rows(w_gateup[:, :FF].astype(jnp.bfloat16), bits, order_a)
    full_up = gather_rows(w_gateup[:, FF:].astype(jnp.bfloat16), bits, order_b)
    gains_f = full_gains.astype(jnp.float32)
    gain_first = gains_f[:D]
    gain_second = gains_f[D : 2 * D]
    gain_mamba = gains_f[2 * D :]
    conv_taps = full_conv.astype(jnp.float32)
    tokens_f = tokens.astype(jnp.float32)
    normed_f, pull_first = jax.vjp(rms_scale, tokens_f, gain_first)
    normed = normed_f.astype(jnp.bfloat16)
    projected = jnp.dot(normed, full_project, preferred_element_type=jnp.float32)
    seq_index = lax.axis_index("seq")
    positions = seq_index * row_count + jnp.arange(row_count, dtype=jnp.int32)
    cosine, sine_table = rope_tables(positions)

    def rope_pair(query_part, key_part):
        return (
            rotate(query_part.reshape(row_count, HEADS, HEAD_DIM), cosine, sine_table),
            rotate(key_part.reshape(row_count, KV_HEADS, HEAD_DIM), cosine, sine_table),
        )

    (query_rot, key_rot), pull_rope = jax.vjp(
        rope_pair, projected[:, :q_width], projected[:, q_width : q_width + kv_width]
    )
    queries = query_rot.astype(jnp.bfloat16).reshape(row_count, KV_HEADS, group_size, HEAD_DIM)
    key_local = key_rot.reshape(row_count, kv_width).astype(jnp.bfloat16)
    value_local = projected[:, q_width + kv_width : offset_cols].astype(jnp.bfloat16)
    key_value = lax.all_gather(
        jnp.concatenate([key_local, value_local], axis=1), "seq", axis=0, tiled=True
    )
    key_all, value_all = key_value[:, :kv_width], key_value[:, kv_width:]

    def scores_for(key_source, shard):
        key_block = lax.dynamic_slice_in_dim(key_source, shard * row_count, row_count, 0)
        key_block = key_block.reshape(row_count, KV_HEADS, HEAD_DIM)
        raw_scores = (
            jnp.einsum("qkgd,skd->kgqs", queries, key_block, preferred_element_type=jnp.float32)
            * scale_factor
        )
        key_pos = shard * row_count + jnp.arange(row_count, dtype=jnp.int32)
        allowed = key_pos[None, :] <= positions[:, None]
        return jnp.where(allowed, raw_scores, -1e30)

    def value_block(value_source, shard):
        picked = lax.dynamic_slice_in_dim(value_source, shard * row_count, row_count, 0)
        return picked.reshape(row_count, KV_HEADS, HEAD_DIM)

    def max_step(shard, carry):
        row_top, row_total = carry
        scores = scores_for(key_all, shard)
        new_top = jnp.maximum(row_top, jnp.max(scores, axis=-1))
        row_total = row_total * jnp.exp(row_top - new_top) + jnp.sum(
            jnp.exp(scores - new_top[..., None]), axis=-1
        )
        return (new_top, row_total)

    start_top = jnp.full((KV_HEADS, group_size, row_count), -1e30, jnp.float32)
    row_top, row_total = lax.fori_loop(
        0, seq_index + 1, max_step, (start_top, jnp.zeros_like(start_top))
    )
    log_total = row_top + jnp.log(row_total)

    def out_step(shard, accum):
        scores = scores_for(key_all, shard)
        probability = jnp.exp(scores - log_total[..., None]).astype(jnp.bfloat16)
        return accum + jnp.einsum(
            "kgqs,skd->qkgd",
            probability,
            value_block(value_all, shard),
            preferred_element_type=jnp.float32,
        )

    attended_f = lax.fori_loop(
        0,
        seq_index + 1,
        out_step,
        jnp.zeros((row_count, KV_HEADS, group_size, HEAD_DIM), jnp.float32),
    )
    attended = (attended_f * out_multiplier).reshape(row_count, q_width).astype(jnp.bfloat16)
    gate_z = projected[:, offset_cols : offset_cols + inner_width]
    xbc_raw = projected[:, offset_cols + inner_width : offset_cols + inner_width + conv_width]
    dt_raw = projected[:, offset_cols + inner_width + conv_width :]
    rim_rows = from_behind(xbc_raw[row_count - (CONV - 1) :], "seq", 1)
    padded = jnp.concatenate([rim_rows, xbc_raw], axis=0)
    (inputs, log_decay, b_matrix, c_matrix, x_heads), pull_prep = jax.vjp(
        prepare, padded, conv_taps, head_params, dt_raw
    )
    (decay_all, end_state), pull_state = jax.vjp(local_state, inputs, log_decay, b_matrix)
    decay_identity = jnp.ones_like(decay_all)
    state_identity = jnp.zeros_like(end_state)
    before_decay, start_state = entering(
        (decay_all, end_state), "seq", chain_step, (decay_identity, state_identity)
    )
    mamba_f, pull_out = jax.vjp(
        mamba_output,
        inputs,
        log_decay,
        b_matrix,
        c_matrix,
        x_heads,
        gate_z,
        head_params,
        gain_mamba,
        start_state,
    )
    joined = jnp.concatenate([attended, mamba_f.astype(jnp.bfloat16)], axis=1)
    hidden = tokens_f + jnp.dot(joined, full_mixout, preferred_element_type=jnp.float32)
    normed2_f, pull_second = jax.vjp(rms_scale, hidden, gain_second)
    normed2 = normed2_f.astype(jnp.bfloat16)
    gate_part = jnp.dot(normed2, full_gate, preferred_element_type=jnp.float32)
    up_part = jnp.dot(normed2, full_up, preferred_element_type=jnp.float32)
    swiglu_out, pull_swiglu = jax.vjp(swiglu, gate_part, up_part)
    activated = swiglu_out.astype(jnp.bfloat16)
    out_block = (hidden + jnp.dot(activated, full_down, preferred_element_type=jnp.float32)).astype(
        jnp.bfloat16
    )
    back_project, back_mixout, back_down = (
        full_project,
        full_mixout,
        full_down,
    )
    grad_out = cotangent.astype(jnp.float32)
    grad_down = jnp.einsum("tf,td->fd", activated, cotangent, preferred_element_type=jnp.float32)
    grad_act = jnp.einsum("td,fd->tf", cotangent, back_down, preferred_element_type=jnp.float32)
    grad_gate_f, grad_up_f = pull_swiglu(grad_act)
    grad_gate_t = grad_gate_f.astype(jnp.bfloat16)
    grad_up_t = grad_up_f.astype(jnp.bfloat16)
    grad_gate = jnp.einsum("tc,tf->cf", normed2, grad_gate_t, preferred_element_type=jnp.float32)
    grad_up = jnp.einsum("tc,tf->cf", normed2, grad_up_t, preferred_element_type=jnp.float32)
    grad_normed2 = jnp.einsum(
        "tf,cf->tc", grad_gate_t, full_gate, preferred_element_type=jnp.float32
    ) + jnp.einsum("tf,cf->tc", grad_up_t, full_up, preferred_element_type=jnp.float32)
    grad_hidden_n, grad_gain_second = pull_second(grad_normed2)
    grad_hidden = grad_out + grad_hidden_n
    grad_branch = grad_hidden.astype(jnp.bfloat16)
    grad_mixout = jnp.einsum("tr,td->rd", joined, grad_branch, preferred_element_type=jnp.float32)
    early = tuple(g.astype(jnp.bfloat16) for g in (grad_down, grad_mixout, grad_gate, grad_up))
    early, grad_branch = lax.optimization_barrier((early, grad_branch))
    own_down = scatter_rows(early[0], bits, order_a).astype(jnp.float32)
    own_mixout = scatter_rows(early[1], bits, order_b).astype(jnp.float32)
    own_gate = scatter_rows(early[2], bits, order_c).astype(jnp.float32)
    own_up = scatter_rows(early[3], bits, order_a).astype(jnp.float32)
    own_gateup = jnp.concatenate([own_gate, own_up], axis=1)
    grad_joined = jnp.einsum(
        "td,rd->tr", grad_branch, back_mixout, preferred_element_type=jnp.float32
    )
    grad_att = (
        grad_joined[:, :q_width]
        .astype(jnp.bfloat16)
        .reshape(row_count, KV_HEADS, group_size, HEAD_DIM)
    )
    grad_mamba = grad_joined[:, q_width:]
    key_back, value_back = (key_all, value_all)
    delta_rows = out_multiplier * jnp.transpose(
        jnp.sum(grad_att.astype(jnp.float32) * attended_f, axis=-1), (1, 2, 0)
    )

    def back_step(shard, carry):
        grad_query, grad_kv = carry
        scores = scores_for(key_back, shard)
        probability = jnp.exp(scores - log_total[..., None])
        value_rows = value_block(value_back, shard)
        key_rows = value_block(key_back, shard)
        grad_probs = out_multiplier * jnp.einsum(
            "qkgd,skd->kgqs", grad_att, value_rows, preferred_element_type=jnp.float32
        )
        grad_scores = (probability * (grad_probs - delta_rows[..., None])).astype(jnp.bfloat16)
        grad_query = grad_query + scale_factor * jnp.einsum(
            "kgqs,skd->qkgd", grad_scores, key_rows, preferred_element_type=jnp.float32
        )
        grad_keys = scale_factor * jnp.einsum(
            "kgqs,qkgd->skd", grad_scores, queries, preferred_element_type=jnp.float32
        )
        grad_values = out_multiplier * jnp.einsum(
            "kgqs,qkgd->skd",
            probability.astype(jnp.bfloat16),
            grad_att,
            preferred_element_type=jnp.float32,
        )
        block_rows = jnp.concatenate(
            [grad_keys.reshape(row_count, kv_width), grad_values.reshape(row_count, kv_width)],
            axis=1,
        )
        grad_kv = lax.dynamic_update_slice_in_dim(grad_kv, block_rows, shard * row_count, 0)
        return (grad_query, grad_kv)

    length_rows = key_back.shape[0]
    grad_query, grad_kv = lax.fori_loop(
        0,
        seq_index + 1,
        back_step,
        (
            jnp.zeros((row_count, KV_HEADS, group_size, HEAD_DIM), jnp.float32),
            jnp.zeros((length_rows, 2 * kv_width), jnp.float32),
        ),
    )
    grad_kv_own = lax.psum_scatter(
        grad_kv.astype(jnp.bfloat16), "seq", scatter_dimension=0, tiled=True
    ).astype(jnp.float32)
    grad_query_pre, grad_key_pre = pull_rope(
        (
            grad_query.reshape(row_count, HEADS, HEAD_DIM),
            grad_kv_own[:, :kv_width].reshape(row_count, KV_HEADS, HEAD_DIM),
        )
    )
    g_inputs, g_logd, g_bmat, g_cmat, g_xheads, g_gate_z, g_head_out, g_gain_mamba, g_start = (
        pull_out(grad_mamba)
    )
    later_decay, carry_grad = entering_2(
        (decay_all, g_start), "seq", chain_step, (decay_identity, state_identity)
    )
    g_decay = jnp.sum(carry_grad * start_state, axis=(1, 2))
    g_inputs_end, g_logd_end, g_bmat_end = pull_state((g_decay, carry_grad))
    g_padded, g_conv, g_head_prep, g_dtraw = pull_prep(
        (g_inputs + g_inputs_end, g_logd + g_logd_end, g_bmat + g_bmat_end, g_cmat, g_xheads)
    )
    back_rim = from_behind(g_padded[: CONV - 1], "seq", -1)
    g_xbc = g_padded[CONV - 1 :]
    g_xbc = jnp.concatenate(
        [g_xbc[: row_count - (CONV - 1)], g_xbc[row_count - (CONV - 1) :] + back_rim], axis=0
    )
    grad_projected = jnp.concatenate(
        [grad_query_pre, grad_key_pre, grad_kv_own[:, kv_width:], g_gate_z, g_xbc, g_dtraw], axis=1
    ).astype(jnp.bfloat16)
    half_cols = offset_cols + inner_width
    grad_project = jnp.einsum(
        "tc,tk->ck", normed, grad_projected, preferred_element_type=jnp.float32
    ).astype(jnp.bfloat16)
    grad_left, grad_right = grad_project[:, :half_cols], grad_project[:, half_cols:]
    grad_normed = jnp.einsum(
        "tk,ck->tc", grad_projected, back_project, preferred_element_type=jnp.float32
    )
    grad_tokens_n, grad_gain_first = pull_first(grad_normed)
    grad_tokens = grad_hidden + grad_tokens_n
    grad_gains = jnp.concatenate([grad_gain_first, grad_gain_second, g_gain_mamba], axis=0)
    own_left = scatter_rows(grad_left.astype(jnp.bfloat16), bits, order_b)
    own_right = scatter_rows(grad_right.astype(jnp.bfloat16), bits, order_c)
    own_project = jnp.concatenate([own_left, own_right], axis=1).astype(jnp.float32)
    head_part = g_head_out + g_head_prep
    vectors = jnp.concatenate([grad_gains, g_conv.reshape(-1), head_part.reshape(-1)])
    vectors = jnp.pad(vectors, (0, -vectors.shape[0] % 1024)).reshape(-1, 128)
    vectors = sum_everywhere(vectors, bits).reshape(-1)
    place = lax.axis_index("batch") * lax.axis_size("seq") + lax.axis_index("seq")
    gain_count, tap_count = grad_gains.shape[0], g_conv.size
    own_gains = lax.dynamic_slice_in_dim(vectors, place * gains.shape[0], gains.shape[0])
    own_conv = lax.dynamic_slice_in_dim(
        vectors[gain_count : gain_count + tap_count].reshape(g_conv.shape),
        place * conv_params.shape[1],
        conv_params.shape[1],
        1,
    )
    grad_head = vectors[gain_count + tap_count : gain_count + tap_count + head_part.size]
    grad_head = grad_head.reshape(head_part.shape)
    r_project = adamw_update(
        w_project, own_project, mom_project, sec_project, rate_matrix, weight_decay
    )
    r_mixout = adamw_update(w_mixout, own_mixout, mom_mixout, sec_mixout, rate_matrix, weight_decay)
    r_gateup = adamw_update(w_gateup, own_gateup, mom_gateup, sec_gateup, rate_matrix, weight_decay)
    r_down = adamw_update(w_down, own_down, mom_down, sec_down, rate_matrix, weight_decay)
    r_gains = adamw_update(gains, own_gains, mom_gains, sec_gains, rate_vector, 0.0)
    r_conv = adamw_update(conv_params, own_conv, mom_conv, sec_conv, rate_vector, 0.0)
    r_head = adamw_update(head_params, grad_head, mom_head, sec_head, rate_vector, 0.0)
    return (
        out_block,
        grad_tokens,
        r_project[0],
        r_project[1],
        r_project[2],
        r_mixout[0],
        r_mixout[1],
        r_mixout[2],
        r_gateup[0],
        r_gateup[1],
        r_gateup[2],
        r_down[0],
        r_down[1],
        r_down[2],
        r_gains[0],
        r_gains[1],
        r_gains[2],
        r_conv[0],
        r_conv[1],
        r_conv[2],
        r_head[0],
        r_head[1],
        r_head[2],
    )


def solution(mesh):
    return jax.shard_map(
        local,
        mesh=mesh,
        in_specs=(
            P(("batch", "seq"), None),
            P(("batch", "seq"), None),
            P(("batch", "seq"), None),
            P(("batch", "seq"), None),
            P(("batch", "seq"), None),
            P(("batch", "seq"), None),
            P(("batch", "seq")),
            P(None, ("batch", "seq")),
            P(),
            P(("batch", "seq"), None),
            P(("batch", "seq"), None),
            P(("batch", "seq"), None),
            P(("batch", "seq"), None),
            P(("batch", "seq"), None),
            P(("batch", "seq"), None),
            P(("batch", "seq"), None),
            P(("batch", "seq"), None),
            P(("batch", "seq")),
            P(("batch", "seq")),
            P(None, ("batch", "seq")),
            P(None, ("batch", "seq")),
            P(),
            P(),
        ),
        out_specs=(
            P(("batch", "seq"), None),
            P(("batch", "seq"), None),
            P(("batch", "seq"), None),
            P(("batch", "seq"), None),
            P(("batch", "seq"), None),
            P(("batch", "seq"), None),
            P(("batch", "seq"), None),
            P(("batch", "seq"), None),
            P(("batch", "seq"), None),
            P(("batch", "seq"), None),
            P(("batch", "seq"), None),
            P(("batch", "seq"), None),
            P(("batch", "seq"), None),
            P(("batch", "seq"), None),
            P(("batch", "seq")),
            P(("batch", "seq")),
            P(("batch", "seq")),
            P(None, ("batch", "seq")),
            P(None, ("batch", "seq")),
            P(None, ("batch", "seq")),
            P(),
            P(),
            P(),
        ),
        check_vma=False,
    )
```
